32 devices in a mesh: pts: 32 (over z, y, x, core).
Axes of the slice: x: 2, y: 2, z: 4, core: 2. Of those that a mesh axis runs over, the one named last changes fastest.
Arguments:
- right_solved: float32 [64, 65536], P(None, 'pts'), may hold values from -6 to 6
- solved_basis_1: bfloat16 [128, 65536], P(None, 'pts'), may hold values from -0.5 to 0.5
- solved_basis_2: bfloat16 [128, 65536], P(None, 'pts'), may hold values from -0.5 to 0.5
- solved_basis_3: bfloat16 [128, 65536], P(None, 'pts'), may hold values from -0.5 to 0.5
- solved_basis_4: bfloat16 [128, 65536], P(None, 'pts'), may hold values from -0.5 to 0.5
- row_basis_1: bfloat16 [128, 65536], P(None, 'pts'), may hold values from -0.03125 to 0.03125
- row_basis_2: bfloat16 [128, 65536], P(None, 'pts'), may hold values from -0.046875 to 0.046875
- row_basis_3: bfloat16 [128, 65536], P(None, 'pts'), may hold values from -0.0625 to 0.0625
- row_basis_4: bfloat16 [128, 65536], P(None, 'pts'), may hold values from -0.09375 to 0.09375
- coupling_1: float32 [256, 256], P('pts'), may hold values from -0.375 to 0.375
- coupling_2: float32 [512, 256], P('pts'), may hold values from -0.375 to 0.375
- coupling_3: float32 [1024, 256], P('pts'), may hold values from -0.375 to 0.375
- coupling_4: float32 [2048, 256], P('pts'), may hold values from -0.375 to 0.375
Outputs:
- solution: float32 [64, 65536], P(None, 'pts')
The draws below stay inside these ranges and needn't reach their ends.
All inputs are finite; a program needn't handle non-finite values.
Results may differ from the reference program's by a relative error of at most 0.0085.
Values may be sent and summed in bfloat16 or wider, within the bound.
No kernel may reach another device: no remote copies, remote signals or barrier semaphores. Data moves between devices by JAX's collectives and lax.ppermute only.
A program may use at most 64 MiB of HBM per device.

```python
import jax
import jax.numpy as jnp
from jax import lax

RANK = 128
NRHS = 64
NPTS = 65536


def block_scale(own_key, dims, split, low, top_value):
    def one(dim, parts):
        draws = jax.random.uniform(jax.random.fold_in(jax.random.fold_in(own_key, 6), dim), (parts,), jnp.float32, low / len(split), top_value / len(split))
        return jnp.repeat(jnp.exp(draws), dims[dim] // parts).reshape((-1,) + (1,) * (len(dims) - dim - 1))

    gain = one(*split[0])
    for cut in split[1:]:
        gain = gain * one(*cut)
    return gain


def centred(stream_key, shape, deviation, limit, shards=(), kind=jnp.bfloat16):
    values = jax.random.normal(stream_key, shape, jnp.float32) * deviation
    if len(shards) > 0:
        values = block_scale(stream_key, shape, shards, -0.22, 0.18) * values
    return jnp.clip(values, min=-limit, max=limit).astype(kind)


def setup_inputs(seed: int = 0) -> dict:
    key_of = jax.random.split(jax.random.key(seed), 14)
    return {
        "right_solved": centred(key_of[0], (NRHS, NPTS), 1.0, 6.0, ((1, 32),), jnp.float32),
        "solved_basis_1": centred(key_of[1], (RANK, NPTS), RANK ** -0.5, 0.5, ((1, 32),)),
        "solved_basis_2": centred(key_of[2], (RANK, NPTS), RANK ** -0.5, 0.5, ((1, 32),)),
        "solved_basis_3": centred(key_of[3], (RANK, NPTS), RANK ** -0.5, 0.5, ((1, 32),)),
        "solved_basis_4": centred(key_of[4], (RANK, NPTS), RANK ** -0.5, 0.5, ((1, 32),)),
        "row_basis_1": centred(key_of[5], (RANK, NPTS), (NPTS // 2) ** -0.5, 0.03125, ((1, 32),)),
        "row_basis_2": centred(key_of[6], (RANK, NPTS), (NPTS // 4) ** -0.5, 0.046875, ((1, 32),)),
        "row_basis_3": centred(key_of[7], (RANK, NPTS), (NPTS // 8) ** -0.5, 0.0625, ((1, 32),)),
        "row_basis_4": centred(key_of[8], (RANK, NPTS), (NPTS // 16) ** -0.5, 0.09375, ((1, 32),)),
        "coupling_1": centred(key_of[9], (2 * RANK, 2 * RANK), (2 * RANK) ** -0.5, 0.375, ((0, 32),), jnp.float32),
        "coupling_2": centred(key_of[10], (4 * RANK, 2 * RANK), (2 * RANK) ** -0.5, 0.375, ((0, 32),), jnp.float32),
        "coupling_3": centred(key_of[11], (8 * RANK, 2 * RANK), (2 * RANK) ** -0.5, 0.375, ((0, 32),), jnp.float32),
        "coupling_4": centred(key_of[12], (16 * RANK, 2 * RANK), (2 * RANK) ** -0.5, 0.375, ((0, 32),), jnp.float32),
    }


def level_apply(current, solved, basis, coupling, level_num):
    kid_count = 2 ** level_num
    total_pts = current.shape[1]
    child_span = total_pts // kid_count
    rounded = current.astype(jnp.bfloat16)
    projected = jnp.einsum("rcp,ncp->crn",
                           basis.reshape(RANK, kid_count, child_span).astype(jnp.float32),
                           rounded.reshape(NRHS, kid_count, child_span).astype(jnp.float32))
    stacked = projected.reshape(kid_count // 2, 2 * RANK, NRHS)
    blocks = coupling.reshape(kid_count // 2, 2 * RANK, 2 * RANK)
    weights = jnp.einsum("kij,kjn->kin", blocks, stacked, precision=lax.Precision.HIGHEST)
    weights_b = weights.astype(jnp.bfloat16).reshape(kid_count, RANK, NRHS)
    correction = jnp.einsum("crn,rcp->ncp", weights_b.astype(jnp.float32),
                            solved.reshape(RANK, kid_count, child_span).astype(jnp.float32))
    return current - correction.reshape(NRHS, total_pts)


def reference(right_solved, solved_basis_1, solved_basis_2, solved_basis_3, solved_basis_4,
              row_basis_1, row_basis_2, row_basis_3, row_basis_4,
              coupling_1, coupling_2, coupling_3, coupling_4):
    solved_all = (solved_basis_1, solved_basis_2, solved_basis_3, solved_basis_4)
    basis_all = (row_basis_1, row_basis_2, row_basis_3, row_basis_4)
    coupling_all = (coupling_1, coupling_2, coupling_3, coupling_4)
    current = right_solved
    for level_num in (4, 3, 2, 1):
        current = level_apply(current, solved_all[level_num - 1], basis_all[level_num - 1],
                              coupling_all[level_num - 1], level_num)
    return current
```

```python
import jax
import jax.numpy as jnp
from jax import lax
from jax.sharding import PartitionSpec as P

BF = jnp.bfloat16
F32 = jnp.float32
LEVELS = (4, 3, 2, 1)


def nn(a, b):
    return lax.dot_general(a, b, (((1,), (0,)), ((), ())), preferred_element_type=F32)


def nt(a, b):
    return lax.dot_general(a, b, (((1,), (1,)), ((), ())), preferred_element_type=F32)


def exchange(parts, bit):
    size = lax.axis_size("pts")
    sent = jnp.concatenate(parts, axis=0)
    got = lax.ppermute(sent, "pts", [(i, i ^ (1 << bit)) for i in range(size)])
    out, start = [], 0
    for part in parts:
        out.append(got[start : start + part.shape[0]])
        start += part.shape[0]
    return out


def on_device(right_solved, s1, s2, s3, s4, r1, r2, r3, r4, c1, c2, c3, c4):
    solved = {1: s1, 2: s2, 3: s3, 4: s4}
    basis = {1: r1, 2: r2, 3: r3, 4: r4}
    rank = s1.shape[0]
    size = lax.axis_size("pts")
    bits = size.bit_length() - 1
    me = lax.axis_index("pts")

    rounded = right_solved.astype(BF)
    proj = {l: nt(rounded, basis[l]) for l in LEVELS}
    gram = {(l, k): nt(solved[l], basis[k]).astype(BF) for l in LEVELS for k in LEVELS if k < l}
    coup = {
        l: (c[:, :rank].astype(BF), c[:, rank:].astype(BF))
        for l, c in ((1, c1), (2, c2), (3, c3), (4, c4))
    }

    current = right_solved
    for bit in range(bits):
        level = bits - bit
        upper = (me >> bit & 1) == 1
        live = [k for k in LEVELS if k <= level]
        pairs = [lk for lk in gram if lk[0] <= level]
        rows_of = [k for k in live if not (level == 1 and k == 1)]
        parts = [proj[k].astype(BF) for k in live]
        parts += [gram[lk] for lk in pairs]
        for k in rows_of:
            parts += list(coup[k])
        got = exchange(parts, bit)
        their_proj = dict(zip(live, got[: len(live)]))
        their_gram = dict(zip(pairs, got[len(live) : len(live) + len(pairs)]))
        rest = got[len(live) + len(pairs) :]
        for i, k in enumerate(rows_of):
            coup[k] = tuple(
                jnp.where(
                    upper,
                    jnp.concatenate([rest[2 * i + h], coup[k][h]], axis=0),
                    jnp.concatenate([coup[k][h], rest[2 * i + h]], axis=0),
                )
                for h in range(2)
            )
        if level in LEVELS:
            own, other = proj[level].astype(BF), their_proj[level]
            left = jnp.where(upper, other, own)
            right = jnp.where(upper, own, other)
            weights = (nt(left, coup[level][0]) + nt(right, coup[level][1])).astype(BF)
            if level == 1:
                mine = weights
            else:
                mine = jnp.where(upper, weights[:, rank:], weights[:, :rank])
                theirs = jnp.where(upper, weights[:, :rank], weights[:, rank:])
            for k in live[1:]:
                proj[k] = (
                    proj[k]
                    + their_proj[k].astype(F32)
                    - nn(mine, gram[level, k])
                    - nn(theirs, their_gram[level, k])
                )
            current = current - nn(mine, solved[level])
        else:
            for k in live:
                proj[k] = proj[k] + their_proj[k].astype(F32)
        for lk in pairs:
            if lk[0] < level:
                gram[lk] = (gram[lk].astype(F32) + their_gram[lk].astype(F32)).astype(BF)
    return current


def solution(mesh):
    wide, tall = P(None, "pts"), P("pts", None)
    return jax.shard_map(
        on_device, mesh=mesh, in_specs=(wide,) * 9 + (tall,) * 4, out_specs=wide, check_vma=False
    )
```

```python
import jax
import jax.numpy as jnp
from jax import lax
from jax.experimental import pallas as pl
from jax.experimental.pallas import tpu as pltpu
from jax.sharding import PartitionSpec as P

BF = jnp.bfloat16
F32 = jnp.float32
LEVELS = (4, 3, 2, 1)
PAIRS = tuple((l, k) for l in LEVELS for k in LEVELS if k < l)
VMEM = pl.BlockSpec(memory_space=pltpu.VMEM)
HBM = pl.BlockSpec(memory_space=pltpu.HBM)


def nn(a, b):
    return lax.dot_general(a, b, (((1,), (0,)), ((), ())), preferred_element_type=F32)


def nt(a, b):
    return lax.dot_general(a, b, (((1,), (1,)), ((), ())), preferred_element_type=F32)


def layout(level, width, rank, rows):
    sizes = {("p", k): width for k in LEVELS if k <= level}
    sizes.update({("g", l, k): rank for l, k in PAIRS if l <= level})
    if level > 1:
        sizes.update({("c", k): 2 * rows[k] for k in LEVELS if k <= level})
    out, start = {}, 0
    for key, size in sizes.items():
        out[key] = (start, start + size)
        start += size
    return out, start


def swap(x, bit):
    size = lax.axis_size("pts")
    return lax.ppermute(x, "pts", [(i, i ^ (1 << bit)) for i in range(size)])


def first_kernel(spans, rank, with_coupling, x_hbm, *refs):
    names = ("r1", "r2", "s4", "s3", "r3", "s2", "r4")
    b_hbm = dict(zip(names, refs[:7]))
    c_refs = dict(zip(LEVELS, refs[7:11])) if with_coupling else {}
    refs = refs[7 + len(c_refs) :]
    out, x_v, b_v = refs[0], refs[1], refs[2]
    sems = refs[3]
    copies = {"x": pltpu.make_async_copy(x_hbm, x_v, sems.at[0])}
    b = {}
    for i, name in enumerate(names):
        b[name] = b_v.at[i]
        copies[name] = pltpu.make_async_copy(b_hbm[name], b[name], sems.at[i + 1])
    for copy in copies.values():
        copy.start()

    def put(key, value):
        out[spans[key][0] : spans[key][1]] = value.astype(BF)

    for k, ref in c_refs.items():
        c = ref[...]
        put(("c", k), jnp.concatenate([c[:, :rank], c[:, rank:]], axis=0))

    copies["x"].wait()
    copies["r1"].wait()
    copies["r2"].wait()
    x = x_v[...].astype(BF)
    low = jnp.concatenate([b["r1"][...], b["r2"][...]], axis=0)
    got = nt(x, low)
    put(("p", 1), got[:, :rank])
    put(("p", 2), got[:, rank:])
    for l, name in ((4, "s4"), (3, "s3")):
        copies[name].wait()
        got = nt(b[name][...], low)
        put(("g", l, 1), got[:, :rank])
        put(("g", l, 2), got[:, rank:])
    copies["r3"].wait()
    put(("g", 4, 3), nt(b["s4"][...], b["r3"][...]))
    copies["s2"].wait()
    put(("g", 2, 1), nt(b["s2"][...], b["r1"][...]))
    copies["r4"].wait()
    got = nt(x, jnp.concatenate([b["r3"][...], b["r4"][...]], axis=0))
    put(("p", 3), got[:, :rank])
    put(("p", 4), got[:, rank:])


def interleave(own, other, upper):
    half = own.shape[0] // 2
    own, other = own.astype(F32), other.astype(F32)
    first = jnp.where(upper, other, own)
    second = jnp.where(upper, own, other)
    return jnp.concatenate([first[:half], second[:half], first[half:], second[half:]], axis=0).astype(BF)


def merge_kernel(bit, spans, then, own, got, out):
    upper = (lax.axis_index("pts") >> bit & 1) == 1
    for key, (lo, hi) in spans.items():
        a, z = own[lo:hi], got[lo:hi]
        if key[0] == "c":
            out[then[key][0] : then[key][1]] = interleave(a, z, upper)
        else:
            out[then[key][0] : then[key][1]] = (a.astype(F32) + z.astype(F32)).astype(BF)


def level_kernel(level, bit, spans, then, rank, own, got, *refs):
    upper = (lax.axis_index("pts") >> bit & 1) == 1
    if level == 1:
        last, weights = refs
    else:
        out, weights = refs[0], refs[1]

    def both(key):
        lo, hi = spans[key]
        return own[lo:hi], got[lo:hi]

    a, z = both(("p", level))
    stacked = jnp.concatenate([jnp.where(upper, z, a), jnp.where(upper, a, z)], axis=1)
    if level == 1:
        c = last[...]
        weights[...] = nt(stacked, jnp.concatenate([c[:rank], c[rank:]], axis=1)).astype(BF)
        return
    a, z = both(("c", level))
    rows = jnp.concatenate(
        [
            jnp.concatenate([a[:rank], a[rank:]], axis=1),
            jnp.concatenate([z[:rank], z[rank:]], axis=1),
        ],
        axis=0,
    )
    w = nt(stacked, rows).astype(BF)
    weights[...] = w[:, :rank]
    below = [k for k in LEVELS if k < level]
    gram = jnp.concatenate([jnp.concatenate(both(("g", level, k)), axis=0) for k in below], axis=1)
    change = nn(w, gram)
    for i, k in enumerate(below):
        a, z = both(("p", k))
        lo, hi = then[("p", k)]
        out[lo:hi] = (a.astype(F32) + z.astype(F32) - change[:, i * rank : (i + 1) * rank]).astype(BF)
    for key in spans:
        if key[0] == "g" and key[1] < level:
            a, z = both(key)
            out[then[key][0] : then[key][1]] = (a.astype(F32) + z.astype(F32)).astype(BF)
        if key[0] == "c" and key[1] < level:
            a, z = both(key)
            rows = interleave(a, z, upper)
            if level == 2:
                refs[2][...] = rows
            else:
                out[then[key][0] : then[key][1]] = rows


def on_device(right_solved, s1, s2, s3, s4, r1, r2, r3, r4, c1, c2, c3, c4):
    solved = {1: s1, 2: s2, 3: s3, 4: s4}
    coupling = {1: c1, 2: c2, 3: c3, 4: c4}
    rank, points = s1.shape
    width = right_solved.shape[0]
    bits = lax.axis_size("pts").bit_length() - 1

    rows = {k: coupling[k].shape[0] for k in LEVELS}
    in_kernel = all(rows[k] % 8 == 0 for k in LEVELS)
    spans, total = layout(4, width, rank, rows)
    inner = total if in_kernel else spans[("c", 4)][0]
    operands = [right_solved, r1, r2, s4, s3, r3, s2, r4]
    if in_kernel:
        operands += [coupling[k] for k in LEVELS]
    operands = [pltpu.with_memory_space_constraint(x, pltpu.HBM) for x in operands]
    buf = pl.pallas_call(
        lambda *refs: first_kernel(spans, rank, in_kernel, *refs),
        out_shape=jax.ShapeDtypeStruct((inner, rank), BF),
        in_specs=[HBM] * 8 + [VMEM] * (len(operands) - 8),
        out_specs=VMEM,
        scratch_shapes=[
            pltpu.VMEM((width, points), F32),
            pltpu.VMEM((7, rank, points), BF),
            pltpu.SemaphoreType.DMA((8,)),
        ],
        compiler_params=pltpu.CompilerParams(vmem_limit_bytes=24 * 2**20),
        name="products",
    )(*operands)

    bit = 0
    if not in_kernel:
        parts = {k: jnp.stack([c[:, :rank], c[:, rank:]]).astype(BF) for k, c in coupling.items()}
        while bits - bit > 4:
            got = swap(buf, bit)
            buf = (buf.astype(F32) + got.astype(F32)).astype(BF)
            upper = (lax.axis_index("pts") >> bit & 1) == 1
            for k in LEVELS:
                got = swap(parts[k], bit)
                first, second = jnp.where(upper, got, parts[k]), jnp.where(upper, parts[k], got)
                parts[k] = jnp.concatenate([first, second], axis=1)
            bit += 1
        rows = {k: parts[k].shape[1] for k in LEVELS}
        buf = jnp.concatenate([buf] + [parts[k].reshape(2 * rows[k], rank) for k in LEVELS], axis=0)
        spans, total = layout(4, width, rank, rows)

    current, last = right_solved, None
    while bit < bits:
        level = bits - bit
        got = swap(buf, bit)
        rows = {k: 2 * rows[k] for k in LEVELS}
        operands, more = [buf, got], []
        if level > 4:
            then, total = layout(4, width, rank, rows)
            kernel = lambda *refs, b=bit, s=spans, t=then: merge_kernel(b, s, t, *refs)
        else:
            then, total = layout(level - 1, width, rank, rows)
            kernel = lambda *refs, l=level, b=bit, s=spans, t=then: level_kernel(l, b, s, t, rank, *refs)
            more = [jax.ShapeDtypeStruct((width, rank), BF)]
        if level == 2:
            more.append(jax.ShapeDtypeStruct((2 * rank, rank), BF))
        if level == 1:
            operands.append(last)
            shapes = more
        else:
            shapes = [jax.ShapeDtypeStruct((total, rank), BF)] + more
        outs = pl.pallas_call(
            kernel,
            out_shape=shapes,
            in_specs=[VMEM] * len(operands),
            out_specs=[VMEM] * len(shapes),
            compiler_params=pltpu.CompilerParams(vmem_limit_bytes=24 * 2**20),
            name="stage",
        )(*operands)
        if level == 2:
            last = outs[2]
        if level <= 4:
            current = current - nn(outs[0 if level == 1 else 1], solved[level])
        buf, spans = outs[0], then
        bit += 1
    return current


def solution(mesh):
    wide, tall = P(None, "pts"), P("pts", None)
    return jax.shard_map(
        on_device, mesh=mesh, in_specs=(wide,) * 9 + (tall,) * 4, out_specs=wide, check_vma=False
    )
```

```python
import jax
import jax.numpy as jnp
from jax import lax
from jax.experimental import pallas as pl
from jax.experimental.pallas import tpu as pltpu
from jax.sharding import PartitionSpec as P

BF = jnp.bfloat16
F32 = jnp.float32
LEVELS = (4, 3, 2, 1)
PAIRS = tuple((l, k) for l in LEVELS for k in LEVELS if k < l)
VMEM = pl.BlockSpec(memory_space=pltpu.VMEM)
HBM = pl.BlockSpec(memory_space=pltpu.HBM)
CHUNKS_IN = 2
CHUNKS_OUT = 4


def nn(a, b):
    return lax.dot_general(a, b, (((1,), (0,)), ((), ())), preferred_element_type=F32)


def nt(a, b):
    return lax.dot_general(a, b, (((1,), (1,)), ((), ())), preferred_element_type=F32)


def layout(level, width, rank, rows):
    sizes = {("p", k): width for k in LEVELS if k <= level}
    sizes.update({("g", l, k): rank for l, k in PAIRS if l <= level})
    if level > 1:
        sizes.update({("c", k): 2 * rows[k] for k in LEVELS if k <= level})
    out, start = {}, 0
    for key, size in sizes.items():
        out[key] = (start, start + size)
        start += size
    return out, start


def swap(x, bit):
    size = lax.axis_size("pts")
    return lax.ppermute(x, "pts", [(i, i ^ (1 << bit)) for i in range(size)])


def first_kernel(spans, rank, width, chunks, with_coupling, x_hbm, *refs):
    b_hbm = dict(zip(("r1", "r2", "s4", "s3", "s2", "r3", "r4"), refs[:7]))
    c_hbm = dict(zip(LEVELS, refs[7:11])) if with_coupling else {}
    refs = refs[7 + len(c_hbm) :]
    out, x_v, left_v, right_v, acc_lo, acc_hi, acc_2, sems, c_sem = refs[:9]
    c_v = dict(zip(LEVELS, refs[9:]))
    points = x_v.shape[1]
    cut = points // chunks
    place = {"s4": (left_v, width), "s3": (left_v, width + rank), "s2": (left_v, width + 2 * rank)}
    place.update({name: (right_v, i * rank) for i, name in enumerate(("r1", "r2", "r3", "r4"))})

    def piece(j, i, name):
        cols = pl.ds(j * cut, cut)
        if name == "x":
            return pltpu.make_async_copy(x_hbm.at[:, cols], x_v.at[:, cols], sems.at[j, i])
        ref, row = place[name]
        return pltpu.make_async_copy(b_hbm[name].at[:, cols], ref.at[pl.ds(row, rank), cols], sems.at[j, i])

    copies = [[piece(j, i, n) for i, n in enumerate(("x", *b_hbm))] for j in range(chunks)]
    c_copies = [pltpu.make_async_copy(c_hbm[k], c_v[k], c_sem.at[i]) for i, k in enumerate(c_hbm)]
    for copy in copies[0] + c_copies:
        copy.start()
    for group in copies[1:]:
        for copy in group:
            copy.start()

    def put(key, value):
        out[spans[key][0] : spans[key][1]] = value.astype(BF)

    for copy in c_copies:
        copy.wait()
    for k, ref in c_v.items():
        c = ref[...]
        put(("c", k), jnp.concatenate([c[:, :rank], c[:, rank:]], axis=0))

    def total(j, ref, value):
        if j > 0:
            value = ref[...] + value
        if j + 1 < chunks:
            ref[...] = value
        return value

    for j in range(chunks):
        for copy in copies[j]:
            copy.wait()
        cols = slice(j * cut, (j + 1) * cut)
        left_v[:width, cols] = x_v[:, cols].astype(BF)
        lo = total(j, acc_lo, nt(left_v[: width + 2 * rank, cols], right_v[: 2 * rank, cols]))
        hi = total(j, acc_hi, nt(left_v[: width + rank, cols], right_v[2 * rank :, cols]))
        two = total(j, acc_2, nt(left_v[width + 2 * rank :, cols], right_v[:rank, cols]))
    for i in range(2):
        side = slice(i * rank, (i + 1) * rank)
        put(("p", 1 + i), lo[:width, side])
        put(("p", 3 + i), hi[:width, side])
        put(("g", 4, 1 + i), lo[width : width + rank, side])
        put(("g", 3, 1 + i), lo[width + rank :, side])
    put(("g", 4, 3), hi[width:, :rank])
    put(("g", 2, 1), two)


def interleave(own, other, upper):
    half = own.shape[0] // 2
    own, other = own.astype(F32), other.astype(F32)
    first = jnp.where(upper, other, own)
    second = jnp.where(upper, own, other)
    return jnp.concatenate([first[:half], second[:half], first[half:], second[half:]], axis=0).astype(BF)


def merge_kernel(bit, spans, then, own, got, out):
    upper = (lax.axis_index("pts") >> bit & 1) == 1
    for key, (lo, hi) in spans.items():
        a, z = own[lo:hi], got[lo:hi]
        if key[0] == "c":
            out[then[key][0] : then[key][1]] = interleave(a, z, upper)
        else:
            out[then[key][0] : then[key][1]] = (a.astype(F32) + z.astype(F32)).astype(BF)


def level_kernel(level, bit, spans, then, rank, own, got, *refs):
    upper = (lax.axis_index("pts") >> bit & 1) == 1
    out, weights = refs[0], refs[1]

    def both(key):
        lo, hi = spans[key]
        return own[lo:hi], got[lo:hi]

    a, z = both(("p", level))
    stacked = jnp.concatenate([jnp.where(upper, z, a), jnp.where(upper, a, z)], axis=1)
    a, z = both(("c", level))
    rows = jnp.concatenate(
        [
            jnp.concatenate([a[:rank], a[rank:]], axis=1),
            jnp.concatenate([z[:rank], z[rank:]], axis=1),
        ],
        axis=0,
    )
    w = nt(stacked, rows).astype(BF)
    weights[...] = w[:, :rank]
    below = [k for k in LEVELS if k < level]
    gram = jnp.concatenate([jnp.concatenate(both(("g", level, k)), axis=0) for k in below], axis=1)
    change = nn(w, gram)
    for i, k in enumerate(below):
        a, z = both(("p", k))
        lo, hi = then[("p", k)]
        out[lo:hi] = (a.astype(F32) + z.astype(F32) - change[:, i * rank : (i + 1) * rank]).astype(BF)
    for key in spans:
        if key[0] == "g" and key[1] < level:
            a, z = both(key)
            out[then[key][0] : then[key][1]] = (a.astype(F32) + z.astype(F32)).astype(BF)
        if key[0] == "c" and key[1] < level:
            a, z = both(key)
            rows = interleave(a, z, upper)
            if level == 2:
                refs[2][...] = rows
            else:
                out[then[key][0] : then[key][1]] = rows


def early_kernel(x_hbm, s4, s3, s2, s1, w4, w3, rest, s2_out, s1_out, s_v, sems):
    rank = s4.shape[0]
    pairs = ((x_hbm, rest), (s4, s_v.at[:rank]), (s3, s_v.at[rank:]), (s2, s2_out), (s1, s1_out))
    copies = [pltpu.make_async_copy(a, z, sems.at[i]) for i, (a, z) in enumerate(pairs)]
    for copy in copies:
        copy.start()
    for copy in copies[:3]:
        copy.wait()
    rest[...] -= nn(jnp.concatenate([w4[...], w3[...]], axis=1), s_v[...])
    for copy in copies[3:]:
        copy.wait()


def middle_kernel(rest, s2, w2, out):
    out[...] = rest[...] - nn(w2[...], s2[...])


def last_kernel(bit, chunks, own, got, coupling, rest, s1, out_hbm, out_v, sems):
    upper = (lax.axis_index("pts") >> bit & 1) == 1
    rank = coupling.shape[0] // 2
    a, z, c = own[...], got[...], coupling[...]
    stacked = jnp.concatenate([jnp.where(upper, z, a), jnp.where(upper, a, z)], axis=1)
    weights = nt(stacked, jnp.concatenate([c[:rank], c[rank:]], axis=1)).astype(BF)
    cut = rest.shape[1] // chunks
    copies = []
    for j in range(chunks):
        cols = slice(j * cut, (j + 1) * cut)
        out_v[:, cols] = rest[:, cols] - nn(weights, s1[:, cols])
        span = pl.ds(j * cut, cut)
        copies.append(pltpu.make_async_copy(out_v.at[:, span], out_hbm.at[:, span], sems.at[j]))
        copies[-1].start()
    for copy in copies:
        copy.wait()


def on_device(right_solved, s1, s2, s3, s4, r1, r2, r3, r4, c1, c2, c3, c4):
    coupling = {1: c1, 2: c2, 3: c3, 4: c4}
    rank, points = s1.shape
    width = right_solved.shape[0]
    bits = lax.axis_size("pts").bit_length() - 1
    params = pltpu.CompilerParams(vmem_limit_bytes=24 * 2**20)

    def stay(x):
        return pltpu.with_memory_space_constraint(x, pltpu.HBM)

    def cost(flops, moved):
        return pl.CostEstimate(flops=flops, bytes_accessed=moved, transcendentals=0)

    rows = {k: coupling[k].shape[0] for k in LEVELS}
    in_kernel = all(rows[k] % 8 == 0 for k in LEVELS)
    spans, total = layout(4, width, rank, rows)
    inner = total if in_kernel else spans[("c", 4)][0]
    operands = [right_solved, r1, r2, s4, s3, s2, r3, r4]
    if in_kernel:
        operands += [coupling[k] for k in LEVELS]
    operands = [stay(x) for x in operands]
    chunks = CHUNKS_IN
    buf = pl.pallas_call(
        lambda *refs: first_kernel(spans, rank, width, chunks, in_kernel, *refs),
        out_shape=jax.ShapeDtypeStruct((inner, rank), BF),
        in_specs=[HBM] * len(operands),
        out_specs=VMEM,
        scratch_shapes=[
            pltpu.VMEM((width, points), F32),
            pltpu.VMEM((width + 3 * rank, points), BF),
            pltpu.VMEM((4 * rank, points), BF),
            pltpu.VMEM((width + 2 * rank, 2 * rank), F32),
            pltpu.VMEM((width + rank, 2 * rank), F32),
            pltpu.VMEM((rank, rank), F32),
            pltpu.SemaphoreType.DMA((chunks, 8)),
            pltpu.SemaphoreType.DMA((4,)),
        ]
        + ([pltpu.VMEM(coupling[k].shape, F32) for k in LEVELS] if in_kernel else []),
        compiler_params=params,
        name="products",
    )(*operands)

    bit = 0
    if not in_kernel:
        parts = {k: jnp.stack([c[:, :rank], c[:, rank:]]).astype(BF) for k, c in coupling.items()}
        while bits - bit > 4:
            got = swap(buf, bit)
            buf = (buf.astype(F32) + got.astype(F32)).astype(BF)
            upper = (lax.axis_index("pts") >> bit & 1) == 1
            for k in LEVELS:
                got = swap(parts[k], bit)
                first, second = jnp.where(upper, got, parts[k]), jnp.where(upper, parts[k], got)
                parts[k] = jnp.concatenate([first, second], axis=1)
            bit += 1
        rows = {k: parts[k].shape[1] for k in LEVELS}
        buf = jnp.concatenate([buf] + [parts[k].reshape(2 * rows[k], rank) for k in LEVELS], axis=0)
        spans, total = layout(4, width, rank, rows)

    weights = {}
    while bits - bit > 1:
        level = bits - bit
        got = swap(buf, bit)
        rows = {k: 2 * rows[k] for k in LEVELS}
        if level > 4:
            then, total = layout(4, width, rank, rows)
            kernel = lambda *refs, b=bit, s=spans, t=then: merge_kernel(b, s, t, *refs)
        else:
            then, total = layout(level - 1, width, rank, rows)
            kernel = lambda *refs, l=level, b=bit, s=spans, t=then: level_kernel(l, b, s, t, rank, *refs)
        shapes = [jax.ShapeDtypeStruct((total, rank), BF)]
        if level <= 4:
            shapes.append(jax.ShapeDtypeStruct((width, rank), BF))
        if level == 2:
            shapes.append(jax.ShapeDtypeStruct((2 * rank, rank), BF))
        outs = pl.pallas_call(
            kernel,
            out_shape=shapes,
            in_specs=[VMEM] * 2,
            out_specs=[VMEM] * len(shapes),
            compiler_params=params,
            name="stage",
        )(buf, got)
        if level <= 4:
            weights[level] = outs[1]
        if level == 3:
            wide = (width, points)
            rest, s2_v, s1_v = pl.pallas_call(
                early_kernel,
                out_shape=[jax.ShapeDtypeStruct(wide, F32)] + [jax.ShapeDtypeStruct((rank, points), BF)] * 2,
                in_specs=[HBM] * 5 + [VMEM] * 2,
                out_specs=[VMEM] * 3,
                scratch_shapes=[pltpu.VMEM((2 * rank, points), BF), pltpu.SemaphoreType.DMA((5,))],
                compiler_params=params,
                cost_estimate=cost(4 * width * rank * points, 6 * width * points + 8 * rank * points),
                name="early",
            )(*[stay(x) for x in (right_solved, s4, s3, s2, s1)], weights[4], weights[3])
        if level == 2:
            rest = pl.pallas_call(
                middle_kernel,
                out_shape=jax.ShapeDtypeStruct(wide, F32),
                in_specs=[VMEM] * 3,
                out_specs=VMEM,
                compiler_params=params,
                cost_estimate=cost(2 * width * rank * points, 8 * width * points),
                name="middle",
            )(rest, s2_v, weights[2])
        buf, spans = outs[0], then
        bit += 1
    got = swap(buf, bit)
    chunks = CHUNKS_OUT
    return pl.pallas_call(
        lambda *refs: last_kernel(bit, chunks, *refs),
        out_shape=jax.ShapeDtypeStruct(wide, F32),
        in_specs=[VMEM] * 5,
        out_specs=HBM,
        scratch_shapes=[pltpu.VMEM(wide, F32), pltpu.SemaphoreType.DMA((chunks,))],
        compiler_params=params,
        name="last",
    )(buf, got, outs[2], rest, s1_v)


def solution(mesh):
    wide, tall = P(None, "pts"), P("pts", None)
    return jax.shard_map(
        on_device, mesh=mesh, in_specs=(wide,) * 9 + (tall,) * 4, out_specs=wide, check_vma=False
    )
```

```python
import functools

import jax
import jax.numpy as jnp
from jax import lax
from jax.experimental import pallas as pl
from jax.experimental.pallas import tpu as pltpu
from jax.sharding import PartitionSpec as P

BF = jnp.bfloat16
F32 = jnp.float32
LEVELS = (4, 3, 2, 1)
VMEM = pl.BlockSpec(memory_space=pltpu.VMEM)
HBM = pl.BlockSpec(memory_space=pltpu.HBM)
CHUNKS_IN = 2
CHUNKS_OUT = 4


def nn(a, b):
    return lax.dot_general(a, b, (((1,), (0,)), ((), ())), preferred_element_type=F32)


def nt(a, b):
    return lax.dot_general(a, b, (((1,), (1,)), ((), ())), preferred_element_type=F32)


def spread(sizes):
    out, start = {}, 0
    for key, size in sizes.items():
        out[key] = (start, start + size)
        start += size
    return out, start


class Plan:
    def __init__(self, width, rank, rows):
        w, r = width, rank

        def start(scale):
            first = {("p", k): w for k in LEVELS}
            first.update({("g", 4, k): r for k in (3, 2, 1)})
            first.update({("c", k): 2 * scale * rows[k] for k in (4, 3)})
            second = {("g", l, k): r for l, k in ((3, 2), (3, 1), (2, 1))}
            second.update({("c", k): 2 * scale * rows[k] for k in (2, 1)})
            return spread(first), spread(second)

        self.device = start(1)
        self.child = start(2)
        self.after_4 = (
            spread({("p", 3): w, ("p", 2): w, ("p", 1): w, ("c", 3): 8 * rows[3]}),
            spread(
                {
                    **{("own", 3, k): r for k in (2, 1)},
                    **{("sib", 3, k): r for k in (2, 1)},
                    ("g", 2, 1): r,
                    **{("c", k, y): 4 * rows[k] for k in (2, 1) for y in (0, 1)},
                }
            ),
        )
        self.before_3 = (
            spread(
                {
                    **{(side, k): w for k in (3, 2, 1) for side in ("own", "sib")},
                    "w4": w,
                    ("own", "c"): 8 * rows[3],
                    ("sib", "c"): 8 * rows[3],
                }
            ),
            spread(
                {
                    **{("own", 3, k): r for k in (2, 1)},
                    **{("sib", 3, k): r for k in (2, 1)},
                    ("g", 2, 1): r,
                    **{("c", k): 16 * rows[k] for k in (2, 1)},
                }
            ),
        )
        self.after_3 = spread(
            {("p", 2): w, ("p", 1): w, ("g", 2, 1): r, **{("c", k): 16 * rows[k] for k in (2, 1)}}
        )

    @staticmethod
    def total(pair):
        return max(pair[0][1], pair[1][1])


def swap(x, even, odd):
    size = lax.axis_size("pts")
    return lax.ppermute(x, "pts", [(i, i ^ (1 << (odd if i & 1 else even))) for i in range(size)])


def index_bit(bit):
    return lax.axis_index("pts") >> bit & 1


def by_role(first, second):
    role = index_bit(0)
    pl.when(role == 0)(first)
    pl.when(role == 1)(second)


def first_kernel(spans, rank, width, chunks, in_kernel, x_hbm, *refs):
    b_hbm = dict(zip(("r1", "r2", "s4", "s3", "s2", "r3", "r4"), refs[:7]))
    c_hbm = dict(zip(LEVELS, refs[7:11])) if in_kernel else {}
    refs = refs[7 + len(c_hbm) :]
    keep, send, x_v, left_v, right_v, acc_lo, acc_hi, acc_2, sems, c_sem = refs[:10]
    c_v = dict(zip(LEVELS, refs[10:]))
    points = x_v.shape[1]
    cut = points // chunks
    place = {"s4": (left_v, width), "s3": (left_v, width + rank), "s2": (left_v, width + 2 * rank)}
    place.update({name: (right_v, i * rank) for i, name in enumerate(("r1", "r2", "r3", "r4"))})

    def piece(j, i, name):
        cols = pl.ds(j * cut, cut)
        if name == "x":
            return pltpu.make_async_copy(x_hbm.at[:, cols], x_v.at[:, cols], sems.at[j, i])
        ref, row = place[name]
        return pltpu.make_async_copy(b_hbm[name].at[:, cols], ref.at[pl.ds(row, rank), cols], sems.at[j, i])

    copies = [[piece(j, i, n) for i, n in enumerate(("x", *b_hbm))] for j in range(chunks)]
    c_copies = [pltpu.make_async_copy(c_hbm[k], c_v[k], c_sem.at[i]) for i, k in enumerate(c_hbm)]
    for copy in copies[0] + c_copies:
        copy.start()
    for group in copies[1:]:
        for copy in group:
            copy.start()

    def add(j, ref, value):
        ref[...] = value if j == 0 else ref[...] + value

    for j in range(chunks):
        for copy in copies[j]:
            copy.wait()
        cols = slice(j * cut, (j + 1) * cut)
        left_v[:width, cols] = x_v[:, cols].astype(BF)
        add(j, acc_lo, nt(left_v[: width + 2 * rank, cols], right_v[: 2 * rank, cols]))
        add(j, acc_hi, nt(left_v[: width + rank, cols], right_v[2 * rank :, cols]))
        add(j, acc_2, nt(left_v[width + 2 * rank :, cols], right_v[:rank, cols]))
    for copy in c_copies:
        copy.wait()

    def write(role_0, role_1):
        def put(key, value):
            for out, table in zip((role_0, role_1), spans):
                if key in table:
                    out[table[key][0] : table[key][1]] = value.astype(BF)

        for i in range(2):
            side = slice(i * rank, (i + 1) * rank)
            put(("p", 1 + i), acc_lo[:width, side])
            put(("p", 3 + i), acc_hi[:width, side])
            put(("g", 4, 1 + i), acc_lo[width : width + rank, side])
            put(("g", 3, 1 + i), acc_lo[width + rank :, side])
        put(("g", 4, 3), acc_hi[width:, :rank])
        put(("g", 2, 1), acc_2[...])
        for k, ref in c_v.items():
            c = ref[...]
            put(("c", k), jnp.concatenate([c[:, :rank], c[:, rank:]], axis=0))

    by_role(lambda: write(keep, send), lambda: write(send, keep))


def interleave(first, second):
    half = first.shape[0] // 2
    if half % 16:
        first, second = first.astype(F32), second.astype(F32)
    parts = [first[:half], second[:half], first[half:], second[half:]]
    return jnp.concatenate(parts, axis=0).astype(BF)


def ordered(own, other, upper):
    return jnp.where(upper, other, own), jnp.where(upper, own, other)


def plus(a, z):
    return (a.astype(F32) + z.astype(F32)).astype(BF)


def merge_kernel(plan, keep, got, out):
    def merge(role):
        for key, (lo, hi) in plan.device[role][0].items():
            a, z = keep[lo:hi], got[lo:hi]
            if key[0] == "c":
                value = interleave(z, a) if role else interleave(a, z)
            else:
                value = plus(a, z)
            lo, hi = plan.child[role][0][key]
            out[lo:hi] = value

    by_role(lambda: merge(0), lambda: merge(1))


def solve(stacked, own_rows, sib_rows, rank):
    sides = [jnp.concatenate([c[:rank], c[rank:]], axis=1) for c in (own_rows, sib_rows)]
    return nt(stacked, jnp.concatenate(sides, axis=0)).astype(BF)


def effect(weights, own_gram, sib_gram):
    gram = [jnp.concatenate([a, z], axis=0) for a, z in zip(own_gram, sib_gram)]
    return nn(weights, jnp.concatenate(gram, axis=1))


def kernel_4(plan, bits, rank, own, got, out, w4):
    def first():
        spans, then = plan.child[0][0], plan.after_4[0][0]

        def both(key):
            lo, hi = spans[key]
            return own[lo:hi], got[lo:hi]

        upper = index_bit(bits - 4) == 1
        stacked = jnp.concatenate(ordered(*both(("p", 4)), upper), axis=1)
        w = solve(stacked, *both(("c", 4)), rank)
        w4[...] = w[:, :rank]
        below = (3, 2, 1)
        pairs = [both(("g", 4, k)) for k in below]
        change = effect(w, [p[0] for p in pairs], [p[1] for p in pairs])
        for i, k in enumerate(below):
            a, z = both(("p", k))
            lo, hi = then[("p", k)]
            out[lo:hi] = (a.astype(F32) + z.astype(F32) - change[:, i * rank : (i + 1) * rank]).astype(BF)
        lo, hi = then[("c", 3)]
        out[lo:hi] = interleave(*ordered(*both(("c", 3)), upper))

    def second():
        spans, then = plan.child[1][0], plan.after_4[1][0]
        upper = index_bit(bits - 3) == 1

        def put(key, value):
            out[then[key][0] : then[key][1]] = value

        for key, (lo, hi) in spans.items():
            a, z = own[lo:hi], got[lo:hi]
            if key[0] == "c":
                for y, value in enumerate(ordered(a, z, upper)):
                    put(("c", key[1], y), value)
            elif key[1] == 3:
                put(("own", *key[1:]), a)
                put(("sib", *key[1:]), z)
            else:
                put(key, plus(a, z))
        w4[...] = jnp.zeros_like(w4)

    by_role(first, second)


def gather_kernel(plan, bits, own, got, w4, out):
    def first():
        spans, then = plan.after_4[0][0], plan.before_3[0][0]
        for key, (lo, hi) in spans.items():
            for side, ref in (("own", own), ("sib", got)):
                to = then[(side, "c" if key[0] == "c" else key[1])]
                out[to[0] : to[1]] = ref[lo:hi]
        out[then["w4"][0] : then["w4"][1]] = w4[...]

    def second():
        spans, then = plan.after_4[1][0], plan.before_3[1][0]
        upper = index_bit(bits - 4) == 1
        for key, (lo, hi) in spans.items():
            if key[0] != "c":
                to = then[key]
                out[to[0] : to[1]] = plus(own[lo:hi], got[lo:hi])
        for k in (2, 1):
            rows = []
            for y in (0, 1):
                lo, hi = spans[("c", k, y)]
                rows.append(interleave(*ordered(own[lo:hi], got[lo:hi], upper)))
            to = then[("c", k)]
            out[to[0] : to[1]] = interleave(*rows)

    by_role(first, second)


def kernel_3(plan, bits, rank, own, got, out, w4, w3):
    def run(a_ref, b_ref):
        a_spans, b_spans, then = plan.before_3[0][0], plan.before_3[1][0], plan.after_3[0]

        def a(key):
            return a_ref[a_spans[key][0] : a_spans[key][1]]

        def b(key):
            return b_ref[b_spans[key][0] : b_spans[key][1]]

        def put(key, value):
            out[then[key][0] : then[key][1]] = value

        upper = index_bit(bits - 3) == 1
        stacked = jnp.concatenate(ordered(a(("own", 3)), a(("sib", 3)), upper), axis=1)
        w = solve(stacked, a(("own", "c")), a(("sib", "c")), rank)
        w3[...] = w[:, :rank]
        w4[...] = a("w4")
        below = (2, 1)
        change = effect(w, [b(("own", 3, k)) for k in below], [b(("sib", 3, k)) for k in below])
        for i, k in enumerate(below):
            total = a(("own", k)).astype(F32) + a(("sib", k)).astype(F32)
            put(("p", k), (total - change[:, i * rank : (i + 1) * rank]).astype(BF))
        for key in (("g", 2, 1), ("c", 2), ("c", 1)):
            put(key, b(key))

    by_role(lambda: run(own, got), lambda: run(got, own))


def kernel_2(plan, bits, rank, own, got, out, w2, last):
    spans = plan.after_3[0]

    def both(key):
        lo, hi = spans[key]
        return own[lo:hi], got[lo:hi]

    upper = index_bit(bits - 2) == 1
    w = solve(jnp.concatenate(ordered(*both(("p", 2)), upper), axis=1), *both(("c", 2)), rank)
    w2[...] = w[:, :rank]
    a, z = both(("p", 1))
    gram = both(("g", 2, 1))
    out[...] = (a.astype(F32) + z.astype(F32) - effect(w, gram[:1], gram[1:])).astype(BF)
    last[...] = interleave(*ordered(*both(("c", 1)), upper))


def early_kernel(x_hbm, s4, s3, s2, s1, w4, w3, rest, s2_out, s1_out, s_v, sems):
    rank = s4.shape[0]
    pairs = ((x_hbm, rest), (s4, s_v.at[:rank]), (s3, s_v.at[rank:]), (s2, s2_out), (s1, s1_out))
    copies = [pltpu.make_async_copy(a, z, sems.at[i]) for i, (a, z) in enumerate(pairs)]
    for copy in copies:
        copy.start()
    for copy in copies[:3]:
        copy.wait()
    rest[...] -= nn(jnp.concatenate([w4[...], w3[...]], axis=1), s_v[...])
    for copy in copies[3:]:
        copy.wait()


def middle_kernel(rest, s2, w2, out):
    out[...] = rest[...] - nn(w2[...], s2[...])


def last_kernel(bits, chunks, own, got, coupling, rest, s1, out_hbm, out_v, sems):
    upper = index_bit(bits - 1) == 1
    rank = coupling.shape[0] // 2
    a, z, c = own[...], got[...], coupling[...]
    stacked = jnp.concatenate(ordered(a, z, upper), axis=1)
    weights = nt(stacked, jnp.concatenate([c[:rank], c[rank:]], axis=1)).astype(BF)
    cut = rest.shape[1] // chunks
    copies = []
    for j in range(chunks):
        cols = slice(j * cut, (j + 1) * cut)
        out_v[:, cols] = rest[:, cols] - nn(weights, s1[:, cols])
        span = pl.ds(j * cut, cut)
        copies.append(pltpu.make_async_copy(out_v.at[:, span], out_hbm.at[:, span], sems.at[j]))
        copies[-1].start()
    for copy in copies:
        copy.wait()


def on_device(right_solved, s1, s2, s3, s4, r1, r2, r3, r4, c1, c2, c3, c4):
    coupling = {1: c1, 2: c2, 3: c3, 4: c4}
    rank, points = s1.shape
    width = right_solved.shape[0]
    bits = lax.axis_size("pts").bit_length() - 1
    params = pltpu.CompilerParams(vmem_limit_bytes=24 * 2**20)

    def stay(x):
        return pltpu.with_memory_space_constraint(x, pltpu.HBM)

    def cost(flops, moved):
        return pl.CostEstimate(flops=flops, bytes_accessed=moved, transcendentals=0)

    def vmem_call(kernel, operands, shapes, name, **more):
        return pl.pallas_call(
            kernel,
            out_shape=shapes,
            in_specs=[VMEM] * len(operands),
            out_specs=[VMEM] * len(shapes),
            compiler_params=params,
            name=name,
            **more,
        )(*operands)

    def buffer(size):
        return jax.ShapeDtypeStruct((size, rank), BF)

    child_bits = bits - 4
    rows = {k: coupling[k].shape[0] for k in LEVELS}
    in_kernel = child_bits == 1 and all(rows[k] % 8 == 0 for k in LEVELS)
    if not in_kernel:
        rows = {k: rows[k] << child_bits - 1 for k in LEVELS}
    plan = Plan(width, rank, rows)
    device = plan.device
    if not in_kernel:
        device = tuple(spread({k: z - a for k, (a, z) in t.items() if k[0] != "c"}) for t, _ in device)
    operands = [right_solved, r1, r2, s4, s3, s2, r3, r4]
    if in_kernel:
        operands += [coupling[k] for k in LEVELS]
    chunks = CHUNKS_IN
    keep, send = pl.pallas_call(
        lambda *refs: first_kernel([t for t, _ in device], rank, width, chunks, in_kernel, *refs),
        out_shape=[buffer(Plan.total(device))] * 2,
        in_specs=[HBM] * len(operands),
        out_specs=[VMEM] * 2,
        scratch_shapes=[
            pltpu.VMEM((width, points), F32),
            pltpu.VMEM((width + 3 * rank, points), BF),
            pltpu.VMEM((4 * rank, points), BF),
            pltpu.VMEM((width + 2 * rank, 2 * rank), F32),
            pltpu.VMEM((width + rank, 2 * rank), F32),
            pltpu.VMEM((rank, rank), F32),
            pltpu.SemaphoreType.DMA((chunks, 8)),
            pltpu.SemaphoreType.DMA((4,)),
        ]
        + ([pltpu.VMEM(coupling[k].shape, F32) for k in LEVELS] if in_kernel else []),
        compiler_params=params,
        name="products",
    )(*[stay(x) for x in operands])

    size = Plan.total(plan.child)
    if in_kernel:
        got = swap(send, 0, 0)
        (buf,) = vmem_call(functools.partial(merge_kernel, plan), (keep, got), [buffer(size)], "merge")
    else:
        both = jnp.stack([keep, send])
        parts = {k: jnp.stack([c[:, :rank], c[:, rank:]]).astype(BF) for k, c in coupling.items()}
        both = plus(both, swap(both[::-1], 0, 0))
        both = jnp.where(index_bit(0) == 1, both[::-1], both)
        for bit in range(child_bits):
            if bit:
                both = plus(both, swap(both, bit, bit))
            upper = index_bit(bit) == 1
            for k in LEVELS:
                got = swap(parts[k], bit, bit)
                parts[k] = jnp.concatenate(ordered(parts[k], got, upper), axis=1)
        shares = []
        for role in (0, 1):
            share = [both[role, : device[role][1]]]
            share += [parts[k].reshape(-1, rank) for k in ((4, 3), (2, 1))[role]]
            share = jnp.concatenate(share, axis=0)
            shares.append(jnp.pad(share, ((0, size - share.shape[0]), (0, 0))))
        buf = jnp.where(index_bit(0) == 1, shares[1], shares[0])

    weight = jax.ShapeDtypeStruct((width, rank), BF)
    got = swap(buf, bits - 4, bits - 3)
    shapes = [buffer(Plan.total(plan.after_4)), weight]
    buf, w4 = vmem_call(functools.partial(kernel_4, plan, bits, rank), (buf, got), shapes, "level_4")
    got = swap(buf, bits - 3, bits - 4)
    shapes = [buffer(Plan.total(plan.before_3))]
    (buf,) = vmem_call(functools.partial(gather_kernel, plan, bits), (buf, got, w4), shapes, "gather")
    got = swap(buf, 0, 0)
    shapes = [buffer(plan.after_3[1]), weight, weight]
    buf, w4, w3 = vmem_call(functools.partial(kernel_3, plan, bits, rank), (buf, got), shapes, "level_3")

    wide = jax.ShapeDtypeStruct((width, points), F32)
    rest, s2_v, s1_v = pl.pallas_call(
        early_kernel,
        out_shape=[wide] + [jax.ShapeDtypeStruct((rank, points), BF)] * 2,
        in_specs=[HBM] * 5 + [VMEM] * 2,
        out_specs=[VMEM] * 3,
        scratch_shapes=[pltpu.VMEM((2 * rank, points), BF), pltpu.SemaphoreType.DMA((5,))],
        compiler_params=params,
        cost_estimate=cost(4 * width * rank * points, 6 * width * points + 8 * rank * points),
        name="early",
    )(*[stay(x) for x in (right_solved, s4, s3, s2, s1)], w4, w3)

    got = swap(buf, bits - 2, bits - 2)
    shapes = [buffer(width), weight, buffer(2 * rank)]
    buf, w2, last = vmem_call(functools.partial(kernel_2, plan, bits, rank), (buf, got), shapes, "level_2")
    (rest,) = vmem_call(
        middle_kernel,
        (rest, s2_v, w2),
        [wide],
        "middle",
        cost_estimate=cost(2 * width * rank * points, 8 * width * points),
    )
    got = swap(buf, bits - 1, bits - 1)
    chunks = CHUNKS_OUT
    return pl.pallas_call(
        functools.partial(last_kernel, bits, chunks),
        out_shape=wide,
        in_specs=[VMEM] * 5,
        out_specs=HBM,
        scratch_shapes=[pltpu.VMEM(wide.shape, F32), pltpu.SemaphoreType.DMA((chunks,))],
        compiler_params=params,
        name="last",
    )(buf, got, last, rest, s1_v)


def solution(mesh):
    wide, tall = P(None, "pts"), P("pts", None)
    return jax.shard_map(
        on_device, mesh=mesh, in_specs=(wide,) * 9 + (tall,) * 4, out_specs=wide, check_vma=False
    )
```

```python
import functools

import jax
import jax.numpy as jnp
from jax import lax
from jax.experimental import pallas as pl
from jax.experimental.pallas import tpu as pltpu
from jax.sharding import PartitionSpec as P

BF = jnp.bfloat16
F32 = jnp.float32
LEVELS = (4, 3, 2, 1)
VMEM = pl.BlockSpec(memory_space=pltpu.VMEM)
HBM = pl.BlockSpec(memory_space=pltpu.HBM)
CHUNKS_IN = 2
CHUNKS_OUT = 4


def nn(a, b):
    return lax.dot_general(a, b, (((1,), (0,)), ((), ())), preferred_element_type=F32)


def nt(a, b):
    return lax.dot_general(a, b, (((1,), (1,)), ((), ())), preferred_element_type=F32)


def tn(a, b):
    return lax.dot_general(a, b, (((0,), (0,)), ((), ())), preferred_element_type=F32)


def spread(sizes):
    out, start = {}, 0
    for key, size in sizes.items():
        out[key] = (start, start + size)
        start += size
    return out, start


class Plan:
    def __init__(self, width, rank, rows):
        w, r = width, rank

        def start(scale):
            first = {("p", k): w for k in LEVELS}
            first.update({("g", 4, k): r for k in (3, 2, 1)})
            first.update({("c", k): 2 * scale * rows[k] for k in (4, 3)})
            second = {("g", l, k): r for l, k in ((3, 2), (3, 1), (2, 1))}
            second.update({("c", k): 2 * scale * rows[k] for k in (2, 1)})
            return spread(first), spread(second)

        self.device = start(1)
        self.child = start(2)
        self.after_4 = (
            spread({("p", 3): w, ("p", 2): w, ("p", 1): w, ("c", 3): 8 * rows[3]}),
            spread(
                {
                    **{("own", 3, k): r for k in (2, 1)},
                    **{("sib", 3, k): r for k in (2, 1)},
                    ("g", 2, 1): r,
                    **{("c", k, y): 4 * rows[k] for k in (2, 1) for y in (0, 1)},
                }
            ),
        )
        self.before_3 = (
            spread(
                {
                    **{(side, k): w for k in (3, 2, 1) for side in ("own", "sib")},
                    "w4": w,
                    ("own", "c"): 8 * rows[3],
                    ("sib", "c"): 8 * rows[3],
                }
            ),
            spread(
                {
                    **{("own", 3, k): r for k in (2, 1)},
                    **{("sib", 3, k): r for k in (2, 1)},
                    ("g", 2, 1): r,
                    **{("c", k): 16 * rows[k] for k in (2, 1)},
                }
            ),
        )
        self.after_3 = spread({("p", 2): w, ("p", 1): w, "h": 2 * r, ("c", 1): 16 * rows[1]})

    @staticmethod
    def total(pair):
        return max(pair[0][1], pair[1][1])


def swap(x, even, odd):
    size = lax.axis_size("pts")
    return lax.ppermute(x, "pts", [(i, i ^ (1 << (odd if i & 1 else even))) for i in range(size)])


def index_bit(bit):
    return lax.axis_index("pts") >> bit & 1


def by_role(first, second):
    role = index_bit(0)
    pl.when(role == 0)(first)
    pl.when(role == 1)(second)


def first_kernel(spans, rank, width, chunks, in_kernel, x_hbm, *refs):
    b_hbm = dict(zip(("r1", "r2", "s4", "s3", "s2", "r3", "r4"), refs[:7]))
    c_hbm = dict(zip(LEVELS, refs[7:11])) if in_kernel else {}
    refs = refs[7 + len(c_hbm) :]
    keep, send, x_v, left_v, right_v, acc_lo, acc_hi, acc_2, sems, c_sem = refs[:10]
    c_v = dict(zip(LEVELS, refs[10:]))
    points = x_v.shape[1]
    cut = points // chunks
    place = {"s4": (left_v, width), "s3": (left_v, width + rank), "s2": (left_v, width + 2 * rank)}
    place.update({name: (right_v, i * rank) for i, name in enumerate(("r1", "r2", "r3", "r4"))})

    def piece(j, i, name):
        cols = pl.ds(j * cut, cut)
        if name == "x":
            return pltpu.make_async_copy(x_hbm.at[:, cols], x_v.at[:, cols], sems.at[j, i])
        ref, row = place[name]
        return pltpu.make_async_copy(b_hbm[name].at[:, cols], ref.at[pl.ds(row, rank), cols], sems.at[j, i])

    copies = [[piece(j, i, n) for i, n in enumerate(("x", *b_hbm))] for j in range(chunks)]
    c_copies = [pltpu.make_async_copy(c_hbm[k], c_v[k], c_sem.at[i]) for i, k in enumerate(c_hbm)]
    for copy in copies[0] + c_copies:
        copy.start()
    for group in copies[1:]:
        for copy in group:
            copy.start()

    def add(j, ref, value):
        ref[...] = value if j == 0 else ref[...] + value

    for j in range(chunks):
        for copy in copies[j]:
            copy.wait()
        cols = slice(j * cut, (j + 1) * cut)
        left_v[:width, cols] = x_v[:, cols].astype(BF)
        add(j, acc_lo, nt(left_v[: width + 2 * rank, cols], right_v[: 2 * rank, cols]))
        add(j, acc_hi, nt(left_v[: width + rank, cols], right_v[2 * rank :, cols]))
        add(j, acc_2, nt(left_v[width + 2 * rank :, cols], right_v[:rank, cols]))
    for copy in c_copies:
        copy.wait()

    def write(role_0, role_1):
        def put(key, value):
            for out, table in zip((role_0, role_1), spans):
                if key in table:
                    out[table[key][0] : table[key][1]] = value.astype(BF)

        for i in range(2):
            side = slice(i * rank, (i + 1) * rank)
            put(("p", 1 + i), acc_lo[:width, side])
            put(("p", 3 + i), acc_hi[:width, side])
            put(("g", 4, 1 + i), acc_lo[width : width + rank, side])
            put(("g", 3, 1 + i), acc_lo[width + rank :, side])
        put(("g", 4, 3), acc_hi[width:, :rank])
        put(("g", 2, 1), acc_2[...])
        for k, ref in c_v.items():
            c = ref[...]
            put(("c", k), jnp.concatenate([c[:, :rank], c[:, rank:]], axis=0))

    by_role(lambda: write(keep, send), lambda: write(send, keep))


def interleave(first, second):
    half = first.shape[0] // 2
    if half % 16:
        first, second = first.astype(F32), second.astype(F32)
    parts = [first[:half], second[:half], first[half:], second[half:]]
    return jnp.concatenate(parts, axis=0).astype(BF)


def ordered(own, other, upper):
    return jnp.where(upper, other, own), jnp.where(upper, own, other)


def plus(a, z):
    return (a.astype(F32) + z.astype(F32)).astype(BF)


def merge_kernel(plan, keep, got, out):
    def merge(role):
        for key, (lo, hi) in plan.device[role][0].items():
            a, z = keep[lo:hi], got[lo:hi]
            if key[0] == "c":
                value = interleave(z, a) if role else interleave(a, z)
            else:
                value = plus(a, z)
            lo, hi = plan.child[role][0][key]
            out[lo:hi] = value

    by_role(lambda: merge(0), lambda: merge(1))


def solve(stacked, own_rows, sib_rows, rank):
    sides = [jnp.concatenate([c[:rank], c[rank:]], axis=1) for c in (own_rows, sib_rows)]
    return nt(stacked, jnp.concatenate(sides, axis=0)).astype(BF)


def effect(weights, own_gram, sib_gram):
    gram = [jnp.concatenate([a, z], axis=0) for a, z in zip(own_gram, sib_gram)]
    return nn(weights, jnp.concatenate(gram, axis=1))


def transfer(rows, gram, rank):
    return jnp.concatenate([tn(rows[:rank], gram), tn(rows[rank:], gram)], axis=0)


def kernel_4(plan, bits, rank, own, got, out, w4):
    def first():
        spans, then = plan.child[0][0], plan.after_4[0][0]

        def both(key):
            lo, hi = spans[key]
            return own[lo:hi], got[lo:hi]

        upper = index_bit(bits - 4) == 1
        stacked = jnp.concatenate(ordered(*both(("p", 4)), upper), axis=1)
        w = solve(stacked, *both(("c", 4)), rank)
        w4[...] = w[:, :rank]
        below = (3, 2, 1)
        pairs = [both(("g", 4, k)) for k in below]
        change = effect(w, [p[0] for p in pairs], [p[1] for p in pairs])
        for i, k in enumerate(below):
            a, z = both(("p", k))
            lo, hi = then[("p", k)]
            out[lo:hi] = (a.astype(F32) + z.astype(F32) - change[:, i * rank : (i + 1) * rank]).astype(BF)
        lo, hi = then[("c", 3)]
        out[lo:hi] = interleave(*ordered(*both(("c", 3)), upper))

    def second():
        spans, then = plan.child[1][0], plan.after_4[1][0]
        upper = index_bit(bits - 3) == 1

        def put(key, value):
            out[then[key][0] : then[key][1]] = value

        for key, (lo, hi) in spans.items():
            a, z = own[lo:hi], got[lo:hi]
            if key[0] == "c":
                for y, value in enumerate(ordered(a, z, upper)):
                    put(("c", key[1], y), value)
            elif key[1] == 3:
                put(("own", *key[1:]), a)
                put(("sib", *key[1:]), z)
            else:
                put(key, plus(a, z))
        w4[...] = jnp.zeros_like(w4)

    by_role(first, second)


def gather_kernel(plan, bits, own, got, w4, out):
    def first():
        spans, then = plan.after_4[0][0], plan.before_3[0][0]
        for key, (lo, hi) in spans.items():
            for side, ref in (("own", own), ("sib", got)):
                to = then[(side, "c" if key[0] == "c" else key[1])]
                out[to[0] : to[1]] = ref[lo:hi]
        out[then["w4"][0] : then["w4"][1]] = w4[...]

    def second():
        spans, then = plan.after_4[1][0], plan.before_3[1][0]
        upper = index_bit(bits - 4) == 1
        for key, (lo, hi) in spans.items():
            if key[0] != "c":
                to = then[key]
                out[to[0] : to[1]] = plus(own[lo:hi], got[lo:hi])
        for k in (2, 1):
            rows = []
            for y in (0, 1):
                lo, hi = spans[("c", k, y)]
                rows.append(interleave(*ordered(own[lo:hi], got[lo:hi], upper)))
            to = then[("c", k)]
            out[to[0] : to[1]] = interleave(*rows)

    by_role(first, second)


def kernel_3(plan, bits, rank, own, got, out, w4, w3, c2):
    def run(a_ref, b_ref):
        a_spans, b_spans, then = plan.before_3[0][0], plan.before_3[1][0], plan.after_3[0]

        def a(key):
            return a_ref[a_spans[key][0] : a_spans[key][1]]

        def b(key):
            return b_ref[b_spans[key][0] : b_spans[key][1]]

        def put(key, value):
            out[then[key][0] : then[key][1]] = value

        upper = index_bit(bits - 3) == 1
        stacked = jnp.concatenate(ordered(a(("own", 3)), a(("sib", 3)), upper), axis=1)
        w = solve(stacked, a(("own", "c")), a(("sib", "c")), rank)
        w3[...] = w[:, :rank]
        w4[...] = a("w4")
        below = (2, 1)
        change = effect(w, [b(("own", 3, k)) for k in below], [b(("sib", 3, k)) for k in below])
        for i, k in enumerate(below):
            total = a(("own", k)).astype(F32) + a(("sib", k)).astype(F32)
            put(("p", k), (total - change[:, i * rank : (i + 1) * rank]).astype(BF))
        put("h", transfer(b(("c", 2)), b(("g", 2, 1)), rank).astype(BF))
        put(("c", 1), b(("c", 1)))
        c2[...] = b(("c", 2))

    by_role(lambda: run(own, got), lambda: run(got, own))


def kernel_2(plan, bits, own, got, early, out, stacked_out, last):
    del early
    spans = plan.after_3[0]

    def both(key):
        lo, hi = spans[key]
        return own[lo:hi], got[lo:hi]

    upper = index_bit(bits - 2) == 1
    stacked = jnp.concatenate(ordered(*both(("p", 2)), upper), axis=1)
    stacked_out[...] = stacked
    a, z = both(("p", 1))
    out[...] = (a.astype(F32) + z.astype(F32) - nn(stacked, plus(*both("h")))).astype(BF)
    last[...] = interleave(*ordered(*both(("c", 1)), upper))


def early_kernel(x_hbm, s4, s3, s2, s1, w4, w3, rest, s2_out, s1_out, s_v, sems):
    rank = s4.shape[0]
    pairs = ((x_hbm, rest), (s4, s_v.at[:rank]), (s3, s_v.at[rank:]), (s2, s2_out), (s1, s1_out))
    copies = [pltpu.make_async_copy(a, z, sems.at[i]) for i, (a, z) in enumerate(pairs)]
    for copy in copies:
        copy.start()
    for copy in copies[:3]:
        copy.wait()
    rest[...] -= nn(jnp.concatenate([w4[...], w3[...]], axis=1), s_v[...])
    for copy in copies[3:]:
        copy.wait()


def middle_kernel(rest, s2, stacked, rows, out):
    rank = s2.shape[0]
    weights = nt(stacked[...], jnp.concatenate([rows[:rank], rows[rank:]], axis=1)).astype(BF)
    out[...] = rest[...] - nn(weights, s2[...])


def last_kernel(bits, chunks, own, got, coupling, rest, s1, out_hbm, out_v, sems):
    upper = index_bit(bits - 1) == 1
    rank = coupling.shape[0] // 2
    a, z, c = own[...], got[...], coupling[...]
    stacked = jnp.concatenate(ordered(a, z, upper), axis=1)
    weights = nt(stacked, jnp.concatenate([c[:rank], c[rank:]], axis=1)).astype(BF)
    cut = rest.shape[1] // chunks
    copies = []
    for j in range(chunks):
        cols = slice(j * cut, (j + 1) * cut)
        out_v[:, cols] = rest[:, cols] - nn(weights, s1[:, cols])
        span = pl.ds(j * cut, cut)
        copies.append(pltpu.make_async_copy(out_v.at[:, span], out_hbm.at[:, span], sems.at[j]))
        copies[-1].start()
    for copy in copies:
        copy.wait()


def on_device(right_solved, s1, s2, s3, s4, r1, r2, r3, r4, c1, c2, c3, c4):
    coupling = {1: c1, 2: c2, 3: c3, 4: c4}
    rank, points = s1.shape
    width = right_solved.shape[0]
    bits = lax.axis_size("pts").bit_length() - 1
    params = pltpu.CompilerParams(vmem_limit_bytes=24 * 2**20)

    def stay(x):
        return pltpu.with_memory_space_constraint(x, pltpu.HBM)

    def cost(flops, moved):
        return pl.CostEstimate(flops=flops, bytes_accessed=moved, transcendentals=0)

    def vmem_call(kernel, operands, shapes, name, **more):
        return pl.pallas_call(
            kernel,
            out_shape=shapes,
            in_specs=[VMEM] * len(operands),
            out_specs=[VMEM] * len(shapes),
            compiler_params=params,
            name=name,
            **more,
        )(*operands)

    def buffer(size):
        return jax.ShapeDtypeStruct((size, rank), BF)

    child_bits = bits - 4
    rows = {k: coupling[k].shape[0] for k in LEVELS}
    in_kernel = child_bits == 1 and all(rows[k] % 8 == 0 for k in LEVELS)
    if not in_kernel:
        rows = {k: rows[k] << child_bits - 1 for k in LEVELS}
    plan = Plan(width, rank, rows)
    device = plan.device
    if not in_kernel:
        device = tuple(spread({k: z - a for k, (a, z) in t.items() if k[0] != "c"}) for t, _ in device)
    operands = [right_solved, r1, r2, s4, s3, s2, r3, r4]
    if in_kernel:
        operands += [coupling[k] for k in LEVELS]
    chunks = CHUNKS_IN
    keep, send = pl.pallas_call(
        lambda *refs: first_kernel([t for t, _ in device], rank, width, chunks, in_kernel, *refs),
        out_shape=[buffer(Plan.total(device))] * 2,
        in_specs=[HBM] * len(operands),
        out_specs=[VMEM] * 2,
        scratch_shapes=[
            pltpu.VMEM((width, points), F32),
            pltpu.VMEM((width + 3 * rank, points), BF),
            pltpu.VMEM((4 * rank, points), BF),
            pltpu.VMEM((width + 2 * rank, 2 * rank), F32),
            pltpu.VMEM((width + rank, 2 * rank), F32),
            pltpu.VMEM((rank, rank), F32),
            pltpu.SemaphoreType.DMA((chunks, 8)),
            pltpu.SemaphoreType.DMA((4,)),
        ]
        + ([pltpu.VMEM(coupling[k].shape, F32) for k in LEVELS] if in_kernel else []),
        compiler_params=params,
        name="products",
    )(*[stay(x) for x in operands])

    size = Plan.total(plan.child)
    if in_kernel:
        got = swap(send, 0, 0)
        (buf,) = vmem_call(functools.partial(merge_kernel, plan), (keep, got), [buffer(size)], "merge")
    else:
        both = jnp.stack([keep, send])
        parts = {k: jnp.stack([c[:, :rank], c[:, rank:]]).astype(BF) for k, c in coupling.items()}
        both = plus(both, swap(both[::-1], 0, 0))
        both = jnp.where(index_bit(0) == 1, both[::-1], both)
        for bit in range(child_bits):
            if bit:
                both = plus(both, swap(both, bit, bit))
            upper = index_bit(bit) == 1
            for k in LEVELS:
                got = swap(parts[k], bit, bit)
                parts[k] = jnp.concatenate(ordered(parts[k], got, upper), axis=1)
        shares = []
        for role in (0, 1):
            share = [both[role, : device[role][1]]]
            share += [parts[k].reshape(-1, rank) for k in ((4, 3), (2, 1))[role]]
            share = jnp.concatenate(share, axis=0)
            shares.append(jnp.pad(share, ((0, size - share.shape[0]), (0, 0))))
        buf = jnp.where(index_bit(0) == 1, shares[1], shares[0])

    weight = jax.ShapeDtypeStruct((width, rank), BF)
    got = swap(buf, bits - 4, bits - 3)
    shapes = [buffer(Plan.total(plan.after_4)), weight]
    buf, w4 = vmem_call(functools.partial(kernel_4, plan, bits, rank), (buf, got), shapes, "level_4")
    got = swap(buf, bits - 3, bits - 4)
    shapes = [buffer(Plan.total(plan.before_3))]
    (buf,) = vmem_call(functools.partial(gather_kernel, plan, bits), (buf, got, w4), shapes, "gather")
    got = swap(buf, 0, 0)
    shapes = [buffer(plan.after_3[1]), weight, weight, buffer(2 * rank)]
    buf, w4, w3, c2_v = vmem_call(functools.partial(kernel_3, plan, bits, rank), (buf, got), shapes, "level_3")

    wide = jax.ShapeDtypeStruct((width, points), F32)
    rest, s2_v, s1_v = pl.pallas_call(
        early_kernel,
        out_shape=[wide] + [jax.ShapeDtypeStruct((rank, points), BF)] * 2,
        in_specs=[HBM] * 5 + [VMEM] * 2,
        out_specs=[VMEM] * 3,
        scratch_shapes=[pltpu.VMEM((2 * rank, points), BF), pltpu.SemaphoreType.DMA((5,))],
        compiler_params=params,
        cost_estimate=cost(4 * width * rank * points, 6 * width * points + 8 * rank * points),
        name="early",
    )(*[stay(x) for x in (right_solved, s4, s3, s2, s1)], w4, w3)

    got = swap(buf, bits - 2, bits - 2)
    shapes = [buffer(width), jax.ShapeDtypeStruct((width, 2 * rank), BF), buffer(2 * rank)]
    buf, stacked, last = vmem_call(functools.partial(kernel_2, plan, bits), (buf, got, s1_v), shapes, "level_2")
    (rest,) = vmem_call(
        middle_kernel,
        (rest, s2_v, stacked, c2_v),
        [wide],
        "middle",
        cost_estimate=cost(2 * width * rank * points, 8 * width * points),
    )
    got = swap(buf, bits - 1, bits - 1)
    chunks = CHUNKS_OUT
    return pl.pallas_call(
        functools.partial(last_kernel, bits, chunks),
        out_shape=wide,
        in_specs=[VMEM] * 5,
        out_specs=HBM,
        scratch_shapes=[pltpu.VMEM(wide.shape, F32), pltpu.SemaphoreType.DMA((chunks,))],
        compiler_params=params,
        name="last",
    )(buf, got, last, rest, s1_v)


def solution(mesh):
    wide, tall = P(None, "pts"), P("pts", None)
    return jax.shard_map(
        on_device, mesh=mesh, in_specs=(wide,) * 9 + (tall,) * 4, out_specs=wide, check_vma=False
    )
```

```python
import functools

import jax
import jax.numpy as jnp
from jax import lax
from jax.experimental import pallas as pl
from jax.experimental.pallas import tpu as pltpu
from jax.sharding import PartitionSpec as P

BF = jnp.bfloat16
F32 = jnp.float32
LEVELS = (4, 3, 2, 1)
SHARES = ((4, 3, 1), (2,))
VMEM = pl.BlockSpec(memory_space=pltpu.VMEM)
HBM = pl.BlockSpec(memory_space=pltpu.HBM)
CHUNKS_IN = 2
PAD = 16
CHUNKS_OUT = 4


def nn(a, b):
    return lax.dot_general(a, b, (((1,), (0,)), ((), ())), preferred_element_type=F32)


def nt(a, b):
    return lax.dot_general(a, b, (((1,), (1,)), ((), ())), preferred_element_type=F32)


def tn(a, b):
    return lax.dot_general(a, b, (((0,), (0,)), ((), ())), preferred_element_type=F32)


def spread(sizes):
    out, start = {}, 0
    for key, size in sizes.items():
        out[key] = (start, start + size)
        start += size
    return out, start


class Plan:
    def __init__(self, width, rank, rows):
        w, r = width, rank

        def start(scale):
            first = {("p", k): w for k in LEVELS}
            first.update({("g", 4, k): r for k in (3, 2, 1)})
            first.update({("c", k): 2 * scale * rows[k] for k in SHARES[0]})
            second = {("g", l, k): r for l, k in ((3, 2), (3, 1), (2, 1))}
            second.update({("c", k): 2 * scale * rows[k] for k in SHARES[1]})
            return spread(first), spread(second)

        self.device = start(1)
        self.child = start(2)
        self.after_4 = (
            spread({("p", 3): w, ("p", 2): w, ("p", 1): w, ("c", 3): 8 * rows[3], ("c", 1): 8 * rows[1]}),
            spread(
                {
                    **{("own", 3, k): r for k in (2, 1)},
                    **{("sib", 3, k): r for k in (2, 1)},
                    ("g", 2, 1): r,
                    **{("c", 2, y): 4 * rows[2] for y in (0, 1)},
                }
            ),
        )
        self.before_3 = (
            spread(
                {
                    **{(side, k): w for k in (3, 2, 1) for side in ("own", "sib")},
                    "w4": w,
                    ("own", "c"): 8 * rows[3],
                    ("sib", "c"): 8 * rows[3],
                }
            ),
            spread(
                {
                    **{("own", 3, k): r for k in (2, 1)},
                    **{("sib", 3, k): r for k in (2, 1)},
                    ("c", 2): 16 * rows[2],
                }
            ),
        )
        self.after_3 = spread({("p", 2): w, ("p", 1): w, "spare": PAD})

    @staticmethod
    def total(pair):
        return max(pair[0][1], pair[1][1])


def swap(x, even, odd):
    size = lax.axis_size("pts")
    return lax.ppermute(x, "pts", [(i, i ^ (1 << (odd if i & 1 else even))) for i in range(size)])


def index_bit(bit):
    return lax.axis_index("pts") >> bit & 1


def by_role(first, second):
    role = index_bit(0)
    pl.when(role == 0)(first)
    pl.when(role == 1)(second)


def first_kernel(spans, rank, width, chunks, in_kernel, x_hbm, *refs):
    b_hbm = dict(zip(("r1", "r2", "s4", "s3", "s2", "r3", "r4"), refs[:7]))
    c_hbm = dict(zip(LEVELS, refs[7:11])) if in_kernel else {}
    refs = refs[7 + len(c_hbm) :]
    keep, send, x_v, left_v, right_v, acc_lo, acc_hi, acc_2, sems, c_sem = refs[:10]
    c_v = dict(zip(LEVELS, refs[10:]))
    points = x_v.shape[1]
    cut = points // chunks
    place = {"s4": (left_v, width), "s3": (left_v, width + rank), "s2": (left_v, width + 2 * rank)}
    place.update({name: (right_v, i * rank) for i, name in enumerate(("r1", "r2", "r3", "r4"))})

    def piece(j, i, name):
        cols = pl.ds(j * cut, cut)
        if name == "x":
            return pltpu.make_async_copy(x_hbm.at[:, cols], x_v.at[:, cols], sems.at[j, i])
        ref, row = place[name]
        return pltpu.make_async_copy(b_hbm[name].at[:, cols], ref.at[pl.ds(row, rank), cols], sems.at[j, i])

    copies = [[piece(j, i, n) for i, n in enumerate(("x", *b_hbm))] for j in range(chunks)]
    c_copies = [pltpu.make_async_copy(c_hbm[k], c_v[k], c_sem.at[i]) for i, k in enumerate(c_hbm)]
    for copy in copies[0] + c_copies:
        copy.start()
    for group in copies[1:]:
        for copy in group:
            copy.start()

    def add(j, ref, value):
        ref[...] = value if j == 0 else ref[...] + value

    for j in range(chunks):
        for copy in copies[j]:
            copy.wait()
        cols = slice(j * cut, (j + 1) * cut)
        left_v[:width, cols] = x_v[:, cols].astype(BF)
        add(j, acc_lo, nt(left_v[: width + 2 * rank, cols], right_v[: 2 * rank, cols]))
        add(j, acc_hi, nt(left_v[: width + rank, cols], right_v[2 * rank :, cols]))
        add(j, acc_2, nt(left_v[width + 2 * rank :, cols], right_v[:rank, cols]))
    for copy in c_copies:
        copy.wait()

    def write(role_0, role_1):
        def put(key, value):
            for out, table in zip((role_0, role_1), spans):
                if key in table:
                    out[table[key][0] : table[key][1]] = value.astype(BF)

        for i in range(2):
            side = slice(i * rank, (i + 1) * rank)
            put(("p", 1 + i), acc_lo[:width, side])
            put(("p", 3 + i), acc_hi[:width, side])
            put(("g", 4, 1 + i), acc_lo[width : width + rank, side])
            put(("g", 3, 1 + i), acc_lo[width + rank :, side])
        put(("g", 4, 3), acc_hi[width:, :rank])
        put(("g", 2, 1), acc_2[...])
        for k, ref in c_v.items():
            c = ref[...]
            put(("c", k), jnp.concatenate([c[:, :rank], c[:, rank:]], axis=0))

    by_role(lambda: write(keep, send), lambda: write(send, keep))


def interleave(first, second):
    half = first.shape[0] // 2
    if half % 16:
        first, second = first.astype(F32), second.astype(F32)
    parts = [first[:half], second[:half], first[half:], second[half:]]
    return jnp.concatenate(parts, axis=0).astype(BF)


def ordered(own, other, upper):
    return jnp.where(upper, other, own), jnp.where(upper, own, other)


def plus(a, z):
    return (a.astype(F32) + z.astype(F32)).astype(BF)


def merge_kernel(plan, keep, got, out):
    def merge(role):
        for key, (lo, hi) in plan.device[role][0].items():
            a, z = keep[lo:hi], got[lo:hi]
            if key[0] == "c":
                value = interleave(z, a) if role else interleave(a, z)
            else:
                value = plus(a, z)
            lo, hi = plan.child[role][0][key]
            out[lo:hi] = value

    by_role(lambda: merge(0), lambda: merge(1))


def solve(stacked, own_rows, sib_rows, rank):
    sides = [jnp.concatenate([c[:rank], c[rank:]], axis=1) for c in (own_rows, sib_rows)]
    return nt(stacked, jnp.concatenate(sides, axis=0)).astype(BF)


def effect(weights, own_gram, sib_gram):
    gram = [jnp.concatenate([a, z], axis=0) for a, z in zip(own_gram, sib_gram)]
    return nn(weights, jnp.concatenate(gram, axis=1))


def transfer(rows, gram, rank):
    return jnp.concatenate([tn(rows[:rank], gram), tn(rows[rank:], gram)], axis=0)


def kernel_4(plan, bits, rank, own, got, after, out, w4):
    del after

    def first():
        spans, then = plan.child[0][0], plan.after_4[0][0]

        def both(key):
            lo, hi = spans[key]
            return own[lo:hi], got[lo:hi]

        upper = index_bit(bits - 4) == 1
        stacked = jnp.concatenate(ordered(*both(("p", 4)), upper), axis=1)
        w = solve(stacked, *both(("c", 4)), rank)
        w4[...] = w[:, :rank]
        below = (3, 2, 1)
        pairs = [both(("g", 4, k)) for k in below]
        change = effect(w, [p[0] for p in pairs], [p[1] for p in pairs])
        for i, k in enumerate(below):
            a, z = both(("p", k))
            lo, hi = then[("p", k)]
            out[lo:hi] = (a.astype(F32) + z.astype(F32) - change[:, i * rank : (i + 1) * rank]).astype(BF)
        for k in (3, 1):
            lo, hi = then[("c", k)]
            out[lo:hi] = interleave(*ordered(*both(("c", k)), upper))

    def second():
        spans, then = plan.child[1][0], plan.after_4[1][0]
        upper = index_bit(bits - 3) == 1

        def put(key, value):
            out[then[key][0] : then[key][1]] = value

        for key, (lo, hi) in spans.items():
            a, z = own[lo:hi], got[lo:hi]
            if key[0] == "c":
                for y, value in enumerate(ordered(a, z, upper)):
                    put(("c", key[1], y), value)
            elif key[1] == 3:
                put(("own", *key[1:]), a)
                put(("sib", *key[1:]), z)
            else:
                put(key, plus(a, z))
        w4[...] = jnp.zeros_like(w4)

    by_role(first, second)


def gather_kernel(plan, bits, own, got, w4, out, gram):
    def first():
        spans, then = plan.after_4[0][0], plan.before_3[0][0]
        for key, (lo, hi) in spans.items():
            if key != ("c", 1):
                for side, ref in (("own", own), ("sib", got)):
                    to = then[(side, "c" if key[0] == "c" else key[1])]
                    out[to[0] : to[1]] = ref[lo:hi]
        out[then["w4"][0] : then["w4"][1]] = w4[...]
        lo, hi = spans[("c", 1)]
        gram[...] = interleave(*ordered(own[lo:hi], got[lo:hi], index_bit(bits - 3) == 1))

    def second():
        spans, then = plan.after_4[1][0], plan.before_3[1][0]
        upper = index_bit(bits - 4) == 1
        for key, (lo, hi) in spans.items():
            if key[0] != "c":
                value = plus(own[lo:hi], got[lo:hi])
                if key in then:
                    out[then[key][0] : then[key][1]] = value
                else:
                    gram[...] = value
        rows = []
        for y in (0, 1):
            lo, hi = spans[("c", 2, y)]
            rows.append(interleave(*ordered(own[lo:hi], got[lo:hi], upper)))
        to = then[("c", 2)]
        out[to[0] : to[1]] = interleave(*rows)

    by_role(first, second)


def early_z_kernel(plan, rank, own, gram, out):
    def first():
        out[:rank] = gram[...]
        out[rank:] = jnp.zeros_like(gram)

    def second():
        lo, hi = plan.before_3[1][0][("c", 2)]
        out[...] = transfer(own[lo:hi], gram[...], rank).astype(BF)

    by_role(first, second)


def meet_z_kernel(bits, rank, own, got, after, *outs):
    del after
    upper = index_bit(bits - 2) == 1

    def put(value):
        for out, rows in zip(outs, (value[:rank], value[rank:])):
            out[...] = rows

    def first():
        put(interleave(*ordered(own[:rank], got[:rank], upper)))

    def second():
        put(plus(own[...], got[...]))

    by_role(first, second)


def shared(mine, other, role):
    own, theirs = [jnp.concatenate([ref[...] for ref in refs], axis=0) for refs in (mine, other)]
    return jnp.where(index_bit(0) == role, own, theirs)


def kernel_3(plan, bits, rank, own, got, after, out, w4, w3, c2):
    del after

    def run(a_ref, b_ref):
        a_spans, b_spans, then = plan.before_3[0][0], plan.before_3[1][0], plan.after_3[0]

        def a(key):
            return a_ref[a_spans[key][0] : a_spans[key][1]]

        def b(key):
            return b_ref[b_spans[key][0] : b_spans[key][1]]

        def put(key, value):
            out[then[key][0] : then[key][1]] = value

        upper = index_bit(bits - 3) == 1
        stacked = jnp.concatenate(ordered(a(("own", 3)), a(("sib", 3)), upper), axis=1)
        w = solve(stacked, a(("own", "c")), a(("sib", "c")), rank)
        put("spare", jnp.zeros((PAD, rank), BF))
        w3[...] = w[:, :rank]
        w4[...] = a("w4")
        below = (2, 1)
        change = effect(w, [b(("own", 3, k)) for k in below], [b(("sib", 3, k)) for k in below])
        for i, k in enumerate(below):
            total = a(("own", k)).astype(F32) + a(("sib", k)).astype(F32)
            put(("p", k), (total - change[:, i * rank : (i + 1) * rank]).astype(BF))
        c2[...] = b(("c", 2))

    by_role(lambda: run(own, got), lambda: run(got, own))


def kernel_2(plan, bits, own, got, m0, m1, o0, o1, out, stacked_out):
    spans = plan.after_3[0]

    def both(key):
        lo, hi = spans[key]
        return own[lo:hi], got[lo:hi]

    stacked = jnp.concatenate(ordered(*both(("p", 2)), index_bit(bits - 2) == 1), axis=1)
    stacked_out[...] = stacked
    effect_1 = shared((m0, m1), (o0, o1), 1)
    a, z = both(("p", 1))
    out[...] = (a.astype(F32) + z.astype(F32) - nn(stacked, effect_1)).astype(BF)


def fetch_kernel(after, *refs):
    del after
    half = len(refs) // 2
    sems = refs[-1]
    copies = [pltpu.make_async_copy(a, z, sems.at[i]) for i, (a, z) in enumerate(zip(refs[:half], refs[half:-1]))]
    for copy in copies:
        copy.start()
    for copy in copies:
        copy.wait()


def early_kernel(rest, s4, s3, w4, w3, out):
    out[...] = rest[...] - nn(w4[...], s4[...]) - nn(w3[...], s3[...])


def middle_kernel(rest, s2, stacked, rows, out):
    rank = s2.shape[0]
    weights = nt(stacked[...], jnp.concatenate([rows[:rank], rows[rank:]], axis=1)).astype(BF)
    out[...] = rest[...] - nn(weights, s2[...])


def last_kernel(bits, chunks, own, got, m0, m1, o0, o1, rest, s1, out_hbm, out_v, sems):
    upper = index_bit(bits - 1) == 1
    rank = m0.shape[0]
    a, z = own[...], got[...]
    c = shared((m0, m1), (o0, o1), 0)
    stacked = jnp.concatenate(ordered(a, z, upper), axis=1)
    weights = nt(stacked, jnp.concatenate([c[:rank], c[rank:]], axis=1)).astype(BF)
    cut = rest.shape[1] // chunks
    copies = []
    for j in range(chunks):
        cols = slice(j * cut, (j + 1) * cut)
        out_v[:, cols] = rest[:, cols] - nn(weights, s1[:, cols])
        span = pl.ds(j * cut, cut)
        copies.append(pltpu.make_async_copy(out_v.at[:, span], out_hbm.at[:, span], sems.at[j]))
        copies[-1].start()
    for copy in copies:
        copy.wait()


def on_device(right_solved, s1, s2, s3, s4, r1, r2, r3, r4, c1, c2, c3, c4):
    coupling = {1: c1, 2: c2, 3: c3, 4: c4}
    rank, points = s1.shape
    width = right_solved.shape[0]
    bits = lax.axis_size("pts").bit_length() - 1
    params = pltpu.CompilerParams(vmem_limit_bytes=24 * 2**20)

    def stay(x):
        return pltpu.with_memory_space_constraint(x, pltpu.HBM)

    def cost(flops, moved):
        return pl.CostEstimate(flops=flops, bytes_accessed=moved, transcendentals=0)

    def vmem_call(kernel, operands, shapes, name, **more):
        return pl.pallas_call(
            kernel,
            out_shape=shapes,
            in_specs=[VMEM] * len(operands),
            out_specs=[VMEM] * len(shapes),
            compiler_params=params,
            name=name,
            **more,
        )(*operands)

    def buffer(size):
        return jax.ShapeDtypeStruct((size, rank), BF)

    child_bits = bits - 4
    rows = {k: coupling[k].shape[0] for k in LEVELS}
    in_kernel = child_bits == 1 and all(rows[k] % 8 == 0 for k in LEVELS)
    if not in_kernel:
        rows = {k: rows[k] << child_bits - 1 for k in LEVELS}
    plan = Plan(width, rank, rows)
    device = plan.device
    if not in_kernel:
        device = tuple(spread({k: z - a for k, (a, z) in t.items() if k[0] != "c"}) for t, _ in device)
    operands = [right_solved, r1, r2, s4, s3, s2, r3, r4]
    if in_kernel:
        operands += [coupling[k] for k in LEVELS]
    chunks = CHUNKS_IN
    keep, send = pl.pallas_call(
        lambda *refs: first_kernel([t for t, _ in device], rank, width, chunks, in_kernel, *refs),
        out_shape=[buffer(Plan.total(device))] * 2,
        in_specs=[HBM] * len(operands),
        out_specs=[VMEM] * 2,
        scratch_shapes=[
            pltpu.VMEM((width, points), F32),
            pltpu.VMEM((width + 3 * rank, points), BF),
            pltpu.VMEM((4 * rank, points), BF),
            pltpu.VMEM((width + 2 * rank, 2 * rank), F32),
            pltpu.VMEM((width + rank, 2 * rank), F32),
            pltpu.VMEM((rank, rank), F32),
            pltpu.SemaphoreType.DMA((chunks, 8)),
            pltpu.SemaphoreType.DMA((4,)),
        ]
        + ([pltpu.VMEM(coupling[k].shape, F32) for k in LEVELS] if in_kernel else []),
        compiler_params=params,
        name="products",
    )(*[stay(x) for x in operands])

    size = Plan.total(plan.child)
    if in_kernel:
        got = swap(send, 0, 0)
        (buf,) = vmem_call(functools.partial(merge_kernel, plan), (keep, got), [buffer(size)], "merge")
    else:
        both = jnp.stack([keep, send])
        parts = {k: jnp.stack([c[:, :rank], c[:, rank:]]).astype(BF) for k, c in coupling.items()}
        both = plus(both, swap(both[::-1], 0, 0))
        both = jnp.where(index_bit(0) == 1, both[::-1], both)
        for bit in range(child_bits):
            if bit:
                both = plus(both, swap(both, bit, bit))
            upper = index_bit(bit) == 1
            for k in LEVELS:
                got = swap(parts[k], bit, bit)
                parts[k] = jnp.concatenate(ordered(parts[k], got, upper), axis=1)
        shares = []
        for role in (0, 1):
            share = [both[role, : device[role][1]]]
            share += [parts[k].reshape(-1, rank) for k in SHARES[role]]
            share = jnp.concatenate(share, axis=0)
            shares.append(jnp.pad(share, ((0, size - share.shape[0]), (0, 0))))
        buf = jnp.where(index_bit(0) == 1, shares[1], shares[0])

    weight = jax.ShapeDtypeStruct((width, rank), BF)
    wide = jax.ShapeDtypeStruct((width, points), F32)
    base = jax.ShapeDtypeStruct((rank, points), BF)
    got = swap(buf, bits - 4, bits - 3)
    rest, s4_v, s3_v, s2_v, s1_v = pl.pallas_call(
        fetch_kernel,
        out_shape=[wide] + [base] * 4,
        in_specs=[VMEM] + [HBM] * 5,
        out_specs=[VMEM] * 5,
        scratch_shapes=[pltpu.SemaphoreType.DMA((5,))],
        compiler_params=params,
        cost_estimate=cost(0, 4 * width * points + 8 * rank * points),
        name="fetch",
    )(buf, *[stay(x) for x in (right_solved, s4, s3, s2, s1)])
    shapes = [buffer(Plan.total(plan.after_4)), weight]
    buf, w4 = vmem_call(functools.partial(kernel_4, plan, bits, rank), (buf, got, s1_v), shapes, "level_4")
    got = swap(buf, bits - 3, bits - 4)
    shapes = [buffer(Plan.total(plan.before_3)), buffer(rank)]
    buf, gram = vmem_call(functools.partial(gather_kernel, plan, bits), (buf, got, w4), shapes, "gather")
    got = swap(buf, 0, 0)
    (own_z,) = vmem_call(functools.partial(early_z_kernel, plan, rank), (buf, gram), [buffer(2 * rank)], "early_z")
    got_z = swap(own_z, bits - 2, bits - 2)
    shapes = [buffer(plan.after_3[1]), weight, weight, buffer(2 * rank)]
    buf, w4, w3, c2_v = vmem_call(functools.partial(kernel_3, plan, bits, rank), (buf, got, own_z), shapes, "level_3")

    got = swap(buf, bits - 2, bits - 2)
    flops, moved = 2 * width * rank * points, 8 * width * points
    (rest,) = vmem_call(early_kernel, (rest, s4_v, s3_v, w4, w3), [wide], "early", cost_estimate=cost(2 * flops, moved))
    meet_z = functools.partial(meet_z_kernel, bits, rank)
    met = vmem_call(meet_z, (own_z, got_z, w3), [buffer(rank)] * 2, "meet_z")
    met = [*met, *[swap(x, 0, 0) for x in met]]
    shapes = [buffer(width), jax.ShapeDtypeStruct((width, 2 * rank), BF)]
    buf, stacked = vmem_call(functools.partial(kernel_2, plan, bits), (buf, got, *met), shapes, "level_2")
    (rest,) = vmem_call(middle_kernel, (rest, s2_v, stacked, c2_v), [wide], "middle", cost_estimate=cost(flops, moved))
    got = swap(buf, bits - 1, bits - 1)
    chunks = CHUNKS_OUT
    return pl.pallas_call(
        functools.partial(last_kernel, bits, chunks),
        out_shape=wide,
        in_specs=[VMEM] * 8,
        out_specs=HBM,
        scratch_shapes=[pltpu.VMEM(wide.shape, F32), pltpu.SemaphoreType.DMA((chunks,))],
        compiler_params=params,
        name="last",
    )(buf, got, *met, rest, s1_v)


def solution(mesh):
    wide, tall = P(None, "pts"), P("pts", None)
    return jax.shard_map(
        on_device, mesh=mesh, in_specs=(wide,) * 9 + (tall,) * 4, out_specs=wide, check_vma=False
    )
```

```python
import functools

import jax
import jax.numpy as jnp
from jax import lax
from jax.experimental import pallas as pl
from jax.experimental.pallas import tpu as pltpu
from jax.sharding import PartitionSpec as P

BF = jnp.bfloat16
F32 = jnp.float32
LEVELS = (4, 3, 2, 1)
LATE = (("c", 3), ("c", 1))
SHARES = ((4, 3, 1), (2,))
VMEM = pl.BlockSpec(memory_space=pltpu.VMEM)
HBM = pl.BlockSpec(memory_space=pltpu.HBM)
CHUNKS_IN = 2
PAD = 16
CHUNKS_OUT = 4


def nn(a, b):
    return lax.dot_general(a, b, (((1,), (0,)), ((), ())), preferred_element_type=F32)


def nt(a, b):
    return lax.dot_general(a, b, (((1,), (1,)), ((), ())), preferred_element_type=F32)


def tn(a, b):
    return lax.dot_general(a, b, (((0,), (0,)), ((), ())), preferred_element_type=F32)


def spread(sizes):
    out, start = {}, 0
    for key, size in sizes.items():
        out[key] = (start, start + size)
        start += size
    return out, start


class Plan:
    def __init__(self, width, rank, rows):
        w, r = width, rank

        def start(scale):
            first = {("p", k): w for k in LEVELS}
            first.update({("g", 4, k): r for k in (3, 2, 1)})
            first.update({("c", k): 2 * scale * rows[k] for k in SHARES[0]})
            second = {("g", l, k): r for l, k in ((3, 2), (3, 1), (2, 1))}
            second.update({("c", k): 2 * scale * rows[k] for k in SHARES[1]})
            return spread(first), spread(second)

        self.device = start(1)
        (first, _), second = start(2)
        late = {key: z - a for key, (a, z) in first.items() if key in LATE}
        self.aside = spread(late)
        self.child = (spread({key: z - a for key, (a, z) in first.items() if key not in LATE}), second)
        self.after_4 = (
            spread({("p", 3): w, ("p", 2): w, ("p", 1): w, ("c", 3): 8 * rows[3], ("c", 1): 8 * rows[1]}),
            spread(
                {
                    **{("own", 3, k): r for k in (2, 1)},
                    **{("sib", 3, k): r for k in (2, 1)},
                    ("g", 2, 1): r,
                    **{("c", 2, y): 4 * rows[2] for y in (0, 1)},
                }
            ),
        )
        self.before_3 = (
            spread(
                {
                    **{(side, k): w for k in (3, 2, 1) for side in ("own", "sib")},
                    "w4": w,
                    ("own", "c"): 8 * rows[3],
                    ("sib", "c"): 8 * rows[3],
                }
            ),
            spread(
                {
                    **{("own", 3, k): r for k in (2, 1)},
                    **{("sib", 3, k): r for k in (2, 1)},
                    ("c", 2): 16 * rows[2],
                }
            ),
        )
        self.after_3 = spread({("p", 2): w, ("p", 1): w, "spare": PAD})

    @staticmethod
    def total(pair):
        return max(pair[0][1], pair[1][1])


def swap(x, even, odd):
    size = lax.axis_size("pts")
    return lax.ppermute(x, "pts", [(i, i ^ (1 << (odd if i & 1 else even))) for i in range(size)])


def index_bit(bit):
    return lax.axis_index("pts") >> bit & 1


def by_role(first, second):
    role = index_bit(0)
    pl.when(role == 0)(first)
    pl.when(role == 1)(second)


def first_kernel(spans, rank, width, chunks, in_kernel, x_hbm, *refs):
    b_hbm = dict(zip(("r1", "r2", "s4", "s3", "s2", "r3", "r4"), refs[:7]))
    c_hbm = dict(zip(LEVELS, refs[7:11])) if in_kernel else {}
    refs = refs[7 + len(c_hbm) :]
    keep, send, x_v, left_v, right_v, acc_lo, acc_hi, acc_2, sems, c_sem = refs[:10]
    c_v = dict(zip(LEVELS, refs[10:]))
    points = x_v.shape[1]
    cut = points // chunks
    place = {"s4": (left_v, width), "s3": (left_v, width + rank), "s2": (left_v, width + 2 * rank)}
    place.update({name: (right_v, i * rank) for i, name in enumerate(("r1", "r2", "r3", "r4"))})

    def piece(j, i, name):
        cols = pl.ds(j * cut, cut)
        if name == "x":
            return pltpu.make_async_copy(x_hbm.at[:, cols], x_v.at[:, cols], sems.at[j, i])
        ref, row = place[name]
        return pltpu.make_async_copy(b_hbm[name].at[:, cols], ref.at[pl.ds(row, rank), cols], sems.at[j, i])

    copies = [[piece(j, i, n) for i, n in enumerate(("x", *b_hbm))] for j in range(chunks)]
    c_copies = [pltpu.make_async_copy(c_hbm[k], c_v[k], c_sem.at[i]) for i, k in enumerate(c_hbm)]
    for copy in copies[0] + c_copies:
        copy.start()
    for group in copies[1:]:
        for copy in group:
            copy.start()

    def add(j, ref, value):
        ref[...] = value if j == 0 else ref[...] + value

    for j in range(chunks):
        for copy in copies[j]:
            copy.wait()
        cols = slice(j * cut, (j + 1) * cut)
        left_v[:width, cols] = x_v[:, cols].astype(BF)
        add(j, acc_lo, nt(left_v[: width + 2 * rank, cols], right_v[: 2 * rank, cols]))
        add(j, acc_hi, nt(left_v[: width + rank, cols], right_v[2 * rank :, cols]))
        add(j, acc_2, nt(left_v[width + 2 * rank :, cols], right_v[:rank, cols]))
    for copy in c_copies:
        copy.wait()

    def write(role_0, role_1):
        def put(key, value):
            for out, table in zip((role_0, role_1), spans):
                if key in table:
                    out[table[key][0] : table[key][1]] = value.astype(BF)

        for i in range(2):
            side = slice(i * rank, (i + 1) * rank)
            put(("p", 1 + i), acc_lo[:width, side])
            put(("p", 3 + i), acc_hi[:width, side])
            put(("g", 4, 1 + i), acc_lo[width : width + rank, side])
            put(("g", 3, 1 + i), acc_lo[width + rank :, side])
        put(("g", 4, 3), acc_hi[width:, :rank])
        put(("g", 2, 1), acc_2[...])
        for k, ref in c_v.items():
            c = ref[...]
            put(("c", k), jnp.concatenate([c[:, :rank], c[:, rank:]], axis=0))

    by_role(lambda: write(keep, send), lambda: write(send, keep))


def interleave(first, second):
    half = first.shape[0] // 2
    if half % 16:
        first, second = first.astype(F32), second.astype(F32)
    parts = [first[:half], second[:half], first[half:], second[half:]]
    return jnp.concatenate(parts, axis=0).astype(BF)


def ordered(own, other, upper):
    return jnp.where(upper, other, own), jnp.where(upper, own, other)


def plus(a, z):
    return (a.astype(F32) + z.astype(F32)).astype(BF)


def merge_kernel(plan, keep, got, out, aside):
    def merge(role):
        for key, (lo, hi) in plan.device[role][0].items():
            a, z = keep[lo:hi], got[lo:hi]
            if key[0] == "c":
                value = interleave(z, a) if role else interleave(a, z)
            else:
                value = plus(a, z)
            late = role == 0 and key in LATE
            lo, hi = (plan.aside if late else plan.child[role])[0][key]
            (aside if late else out)[lo:hi] = value
        if role:
            aside[...] = jnp.zeros_like(aside)

    by_role(lambda: merge(0), lambda: merge(1))


def solve(stacked, own_rows, sib_rows, rank):
    sides = [jnp.concatenate([c[:rank], c[rank:]], axis=1) for c in (own_rows, sib_rows)]
    return nt(stacked, jnp.concatenate(sides, axis=0)).astype(BF)


def effect(weights, own_gram, sib_gram):
    gram = [jnp.concatenate([a, z], axis=0) for a, z in zip(own_gram, sib_gram)]
    return nn(weights, jnp.concatenate(gram, axis=1))


def transfer(rows, gram, rank):
    return jnp.concatenate([tn(rows[:rank], gram), tn(rows[rank:], gram)], axis=0)


def kernel_4(plan, bits, rank, own, got, after, out, w4):
    del after

    def first():
        spans, then = plan.child[0][0], plan.after_4[0][0]

        def both(key):
            lo, hi = spans[key]
            return own[lo:hi], got[lo:hi]

        upper = index_bit(bits - 4) == 1
        stacked = jnp.concatenate(ordered(*both(("p", 4)), upper), axis=1)
        w = solve(stacked, *both(("c", 4)), rank)
        w4[...] = w[:, :rank]
        below = (3, 2, 1)
        pairs = [both(("g", 4, k)) for k in below]
        change = effect(w, [p[0] for p in pairs], [p[1] for p in pairs])
        for i, k in enumerate(below):
            a, z = both(("p", k))
            lo, hi = then[("p", k)]
            out[lo:hi] = (a.astype(F32) + z.astype(F32) - change[:, i * rank : (i + 1) * rank]).astype(BF)

    def second():
        spans, then = plan.child[1][0], plan.after_4[1][0]
        upper = index_bit(bits - 3) == 1

        def put(key, value):
            out[then[key][0] : then[key][1]] = value

        for key, (lo, hi) in spans.items():
            a, z = own[lo:hi], got[lo:hi]
            if key[0] == "c":
                for y, value in enumerate(ordered(a, z, upper)):
                    put(("c", key[1], y), value)
            elif key[1] == 3:
                put(("own", *key[1:]), a)
                put(("sib", *key[1:]), z)
            else:
                put(key, plus(a, z))
        w4[...] = jnp.zeros_like(w4)

    by_role(first, second)


def place_kernel(plan, bits, before, own, got, out):
    del before

    def first():
        for key, (lo, hi) in plan.aside[0].items():
            value = interleave(*ordered(own[lo:hi], got[lo:hi], index_bit(bits - 4) == 1))
            lo, hi = plan.after_4[0][0][key]
            out[lo:hi] = value

    pl.when(index_bit(0) == 0)(first)


def gather_kernel(plan, bits, own, got, w4, out, gram):
    def first():
        spans, then = plan.after_4[0][0], plan.before_3[0][0]
        for key, (lo, hi) in spans.items():
            if key != ("c", 1):
                for side, ref in (("own", own), ("sib", got)):
                    to = then[(side, "c" if key[0] == "c" else key[1])]
                    out[to[0] : to[1]] = ref[lo:hi]
        out[then["w4"][0] : then["w4"][1]] = w4[...]
        lo, hi = spans[("c", 1)]
        gram[...] = interleave(*ordered(own[lo:hi], got[lo:hi], index_bit(bits - 3) == 1))

    def second():
        spans, then = plan.after_4[1][0], plan.before_3[1][0]
        upper = index_bit(bits - 4) == 1
        for key, (lo, hi) in spans.items():
            if key[0] != "c":
                value = plus(own[lo:hi], got[lo:hi])
                if key in then:
                    out[then[key][0] : then[key][1]] = value
                else:
                    gram[...] = value
        rows = []
        for y in (0, 1):
            lo, hi = spans[("c", 2, y)]
            rows.append(interleave(*ordered(own[lo:hi], got[lo:hi], upper)))
        to = then[("c", 2)]
        out[to[0] : to[1]] = interleave(*rows)

    by_role(first, second)


def early_z_kernel(plan, rank, own, gram, out):
    def first():
        out[:rank] = gram[...]
        out[rank:] = jnp.zeros_like(gram)

    def second():
        lo, hi = plan.before_3[1][0][("c", 2)]
        out[...] = transfer(own[lo:hi], gram[...], rank).astype(BF)

    by_role(first, second)


def meet_z_kernel(bits, rank, own, got, after, *outs):
    del after
    upper = index_bit(bits - 2) == 1

    def put(value):
        for out, rows in zip(outs, (value[:rank], value[rank:])):
            out[...] = rows

    def first():
        put(interleave(*ordered(own[:rank], got[:rank], upper)))

    def second():
        put(plus(own[...], got[...]))

    by_role(first, second)


def shared(mine, other, role):
    own, theirs = [jnp.concatenate([ref[...] for ref in refs], axis=0) for refs in (mine, other)]
    return jnp.where(index_bit(0) == role, own, theirs)


def kernel_3(plan, bits, rank, own, got, after, out, w4, w3, c2):
    del after

    def run(a_ref, b_ref):
        a_spans, b_spans, then = plan.before_3[0][0], plan.before_3[1][0], plan.after_3[0]

        def a(key):
            return a_ref[a_spans[key][0] : a_spans[key][1]]

        def b(key):
            return b_ref[b_spans[key][0] : b_spans[key][1]]

        def put(key, value):
            out[then[key][0] : then[key][1]] = value

        upper = index_bit(bits - 3) == 1
        stacked = jnp.concatenate(ordered(a(("own", 3)), a(("sib", 3)), upper), axis=1)
        w = solve(stacked, a(("own", "c")), a(("sib", "c")), rank)
        put("spare", jnp.zeros((PAD, rank), BF))
        w3[...] = w[:, :rank]
        w4[...] = a("w4")
        below = (2, 1)
        change = effect(w, [b(("own", 3, k)) for k in below], [b(("sib", 3, k)) for k in below])
        for i, k in enumerate(below):
            total = a(("own", k)).astype(F32) + a(("sib", k)).astype(F32)
            put(("p", k), (total - change[:, i * rank : (i + 1) * rank]).astype(BF))
        c2[...] = b(("c", 2))

    by_role(lambda: run(own, got), lambda: run(got, own))


def kernel_2(plan, bits, own, got, m0, m1, o0, o1, out, stacked_out):
    spans = plan.after_3[0]

    def both(key):
        lo, hi = spans[key]
        return own[lo:hi], got[lo:hi]

    stacked = jnp.concatenate(ordered(*both(("p", 2)), index_bit(bits - 2) == 1), axis=1)
    stacked_out[...] = stacked
    effect_1 = shared((m0, m1), (o0, o1), 1)
    a, z = both(("p", 1))
    out[...] = (a.astype(F32) + z.astype(F32) - nn(stacked, effect_1)).astype(BF)


def fetch_kernel(after, *refs):
    del after
    half = len(refs) // 2
    sems = refs[-1]
    copies = [pltpu.make_async_copy(a, z, sems.at[i]) for i, (a, z) in enumerate(zip(refs[:half], refs[half:-1]))]
    for copy in copies:
        copy.start()
    for copy in copies:
        copy.wait()


def early_kernel(rest, s4, s3, w4, w3, out):
    out[...] = rest[...] - nn(w4[...], s4[...]) - nn(w3[...], s3[...])


def middle_kernel(rest, s2, stacked, rows, out):
    rank = s2.shape[0]
    weights = nt(stacked[...], jnp.concatenate([rows[:rank], rows[rank:]], axis=1)).astype(BF)
    out[...] = rest[...] - nn(weights, s2[...])


def basis_kernel(m0, m1, o0, o1, s1, out):
    rank = m0.shape[0]
    c = shared((m0, m1), (o0, o1), 0)
    out[:rank] = tn(c[:rank], s1[...]).astype(BF)
    out[rank:] = tn(c[rank:], s1[...]).astype(BF)


def last_kernel(bits, chunks, own, got, rest, basis, out_hbm, out_v, sems):
    upper = index_bit(bits - 1) == 1
    stacked = jnp.concatenate(ordered(own[...], got[...], upper), axis=1)
    cut = rest.shape[1] // chunks
    copies = []
    for j in range(chunks):
        cols = slice(j * cut, (j + 1) * cut)
        out_v[:, cols] = rest[:, cols] - nn(stacked, basis[:, cols])
        span = pl.ds(j * cut, cut)
        copies.append(pltpu.make_async_copy(out_v.at[:, span], out_hbm.at[:, span], sems.at[j]))
        copies[-1].start()
    for copy in copies:
        copy.wait()


def on_device(right_solved, s1, s2, s3, s4, r1, r2, r3, r4, c1, c2, c3, c4):
    coupling = {1: c1, 2: c2, 3: c3, 4: c4}
    rank, points = s1.shape
    width = right_solved.shape[0]
    bits = lax.axis_size("pts").bit_length() - 1
    params = pltpu.CompilerParams(vmem_limit_bytes=24 * 2**20)

    def stay(x):
        return pltpu.with_memory_space_constraint(x, pltpu.HBM)

    def cost(flops, moved):
        return pl.CostEstimate(flops=flops, bytes_accessed=moved, transcendentals=0)

    def vmem_call(kernel, operands, shapes, name, **more):
        return pl.pallas_call(
            kernel,
            out_shape=shapes,
            in_specs=[VMEM] * len(operands),
            out_specs=[VMEM] * len(shapes),
            compiler_params=params,
            name=name,
            **more,
        )(*operands)

    def buffer(size):
        return jax.ShapeDtypeStruct((size, rank), BF)

    child_bits = bits - 4
    rows = {k: coupling[k].shape[0] for k in LEVELS}
    in_kernel = child_bits == 1 and all(rows[k] % 8 == 0 for k in LEVELS)
    if not in_kernel:
        rows = {k: rows[k] << child_bits - 1 for k in LEVELS}
    plan = Plan(width, rank, rows)
    device = plan.device
    if not in_kernel:
        device = tuple(spread({k: z - a for k, (a, z) in t.items() if k[0] != "c"}) for t, _ in device)
    operands = [right_solved, r1, r2, s4, s3, s2, r3, r4]
    if in_kernel:
        operands += [coupling[k] for k in LEVELS]
    chunks = CHUNKS_IN
    keep, send = pl.pallas_call(
        lambda *refs: first_kernel([t for t, _ in device], rank, width, chunks, in_kernel, *refs),
        out_shape=[buffer(Plan.total(device))] * 2,
        in_specs=[HBM] * len(operands),
        out_specs=[VMEM] * 2,
        scratch_shapes=[
            pltpu.VMEM((width, points), F32),
            pltpu.VMEM((width + 3 * rank, points), BF),
            pltpu.VMEM((4 * rank, points), BF),
            pltpu.VMEM((width + 2 * rank, 2 * rank), F32),
            pltpu.VMEM((width + rank, 2 * rank), F32),
            pltpu.VMEM((rank, rank), F32),
            pltpu.SemaphoreType.DMA((chunks, 8)),
            pltpu.SemaphoreType.DMA((4,)),
        ]
        + ([pltpu.VMEM(coupling[k].shape, F32) for k in LEVELS] if in_kernel else []),
        compiler_params=params,
        name="products",
    )(*[stay(x) for x in operands])

    size = Plan.total(plan.child)
    if in_kernel:
        got = swap(send, 0, 0)
        shapes = [buffer(size), buffer(plan.aside[1])]
        buf, aside = vmem_call(functools.partial(merge_kernel, plan), (keep, got), shapes, "merge")
    else:
        both = jnp.stack([keep, send])
        parts = {k: jnp.stack([c[:, :rank], c[:, rank:]]).astype(BF) for k, c in coupling.items()}
        both = plus(both, swap(both[::-1], 0, 0))
        both = jnp.where(index_bit(0) == 1, both[::-1], both)
        for bit in range(child_bits):
            if bit:
                both = plus(both, swap(both, bit, bit))
            upper = index_bit(bit) == 1
            for k in LEVELS:
                got = swap(parts[k], bit, bit)
                parts[k] = jnp.concatenate(ordered(parts[k], got, upper), axis=1)
        shares = []
        for role in (0, 1):
            share = [both[role, : device[role][1]]]
            share += [parts[k].reshape(-1, rank) for k in SHARES[role] if ("c", k) not in LATE]
            share = jnp.concatenate(share, axis=0)
            shares.append(jnp.pad(share, ((0, size - share.shape[0]), (0, 0))))
        buf = jnp.where(index_bit(0) == 1, shares[1], shares[0])
        aside = jnp.concatenate([parts[k].reshape(-1, rank) for _, k in LATE], axis=0)

    weight = jax.ShapeDtypeStruct((width, rank), BF)
    wide = jax.ShapeDtypeStruct((width, points), F32)
    base = jax.ShapeDtypeStruct((rank, points), BF)
    got = swap(buf, bits - 4, bits - 3)
    got_aside = swap(aside, bits - 4, bits - 3)
    rest, s4_v, s3_v, s2_v, s1_v = pl.pallas_call(
        fetch_kernel,
        out_shape=[wide] + [base] * 4,
        in_specs=[VMEM] + [HBM] * 5,
        out_specs=[VMEM] * 5,
        scratch_shapes=[pltpu.SemaphoreType.DMA((5,))],
        compiler_params=params,
        cost_estimate=cost(0, 4 * width * points + 8 * rank * points),
        name="fetch",
    )(buf, *[stay(x) for x in (right_solved, s4, s3, s2, s1)])
    shapes = [buffer(Plan.total(plan.after_4)), weight]
    buf, w4 = vmem_call(functools.partial(kernel_4, plan, bits, rank), (buf, got, s1_v), shapes, "level_4")
    place = functools.partial(place_kernel, plan, bits)
    (buf,) = vmem_call(place, (buf, aside, got_aside), [buffer(Plan.total(plan.after_4))], "place", input_output_aliases={0: 0})
    got = swap(buf, bits - 3, bits - 4)
    shapes = [buffer(Plan.total(plan.before_3)), buffer(rank)]
    buf, gram = vmem_call(functools.partial(gather_kernel, plan, bits), (buf, got, w4), shapes, "gather")
    got = swap(buf, 0, 0)
    (own_z,) = vmem_call(functools.partial(early_z_kernel, plan, rank), (buf, gram), [buffer(2 * rank)], "early_z")
    got_z = swap(own_z, bits - 2, bits - 2)
    shapes = [buffer(plan.after_3[1]), weight, weight, buffer(2 * rank)]
    buf, w4, w3, c2_v = vmem_call(functools.partial(kernel_3, plan, bits, rank), (buf, got, own_z), shapes, "level_3")

    got = swap(buf, bits - 2, bits - 2)
    flops, moved = 2 * width * rank * points, 8 * width * points
    (rest,) = vmem_call(early_kernel, (rest, s4_v, s3_v, w4, w3), [wide], "early", cost_estimate=cost(2 * flops, moved))
    meet_z = functools.partial(meet_z_kernel, bits, rank)
    met = vmem_call(meet_z, (own_z, got_z, w3), [buffer(rank)] * 2, "meet_z")
    met = [*met, *[swap(x, 0, 0) for x in met]]
    shapes = [buffer(width), jax.ShapeDtypeStruct((width, 2 * rank), BF)]
    buf, stacked = vmem_call(functools.partial(kernel_2, plan, bits), (buf, got, *met), shapes, "level_2")
    (rest,) = vmem_call(middle_kernel, (rest, s2_v, stacked, c2_v), [wide], "middle", cost_estimate=cost(flops, moved))
    wide_basis = jax.ShapeDtypeStruct((2 * rank, points), BF)
    (basis_1,) = vmem_call(basis_kernel, (*met, s1_v), [wide_basis], "basis_1", cost_estimate=cost(4 * rank * rank * points, 6 * rank * points))
    got = swap(buf, bits - 1, bits - 1)
    chunks = CHUNKS_OUT
    return pl.pallas_call(
        functools.partial(last_kernel, bits, chunks),
        out_shape=wide,
        in_specs=[VMEM] * 4,
        out_specs=HBM,
        scratch_shapes=[pltpu.VMEM(wide.shape, F32), pltpu.SemaphoreType.DMA((chunks,))],
        compiler_params=params,
        name="last",
    )(buf, got, rest, basis_1)


def solution(mesh):
    wide, tall = P(None, "pts"), P("pts", None)
    return jax.shard_map(
        on_device, mesh=mesh, in_specs=(wide,) * 9 + (tall,) * 4, out_specs=wide, check_vma=False
    )
```

```python
import functools

import jax
import jax.numpy as jnp
from jax import lax
from jax.experimental import pallas as pl
from jax.experimental.pallas import tpu as pltpu
from jax.sharding import PartitionSpec as P

BF = jnp.bfloat16
F32 = jnp.float32
LEVELS = (4, 3, 2, 1)
LATE = (("p", 2), ("p", 1), ("g", 4, 2), ("g", 4, 1))
SHARES = ((4, 3, 1), (2,))
VMEM = pl.BlockSpec(memory_space=pltpu.VMEM)
HBM = pl.BlockSpec(memory_space=pltpu.HBM)
CHUNKS_IN = 2
PAD = 16
CHUNKS_OUT = 4


def nn(a, b):
    return lax.dot_general(a, b, (((1,), (0,)), ((), ())), preferred_element_type=F32)


def nt(a, b):
    return lax.dot_general(a, b, (((1,), (1,)), ((), ())), preferred_element_type=F32)


def tn(a, b):
    return lax.dot_general(a, b, (((0,), (0,)), ((), ())), preferred_element_type=F32)


def spread(sizes):
    out, start = {}, 0
    for key, size in sizes.items():
        out[key] = (start, start + size)
        start += size
    return out, start


class Plan:
    def __init__(self, width, rank, rows):
        w, r = width, rank

        def start(scale):
            first = {("p", k): w for k in LEVELS}
            first.update({("g", 4, k): r for k in (3, 2, 1)})
            first.update({("c", k): 2 * scale * rows[k] for k in SHARES[0]})
            second = {("g", l, k): r for l, k in ((3, 2), (3, 1), (2, 1))}
            second.update({("c", k): 2 * scale * rows[k] for k in SHARES[1]})
            return spread(first), spread(second)

        self.device = start(1)
        (first, _), second = start(2)
        late = {key: z - a for key, (a, z) in first.items() if key in LATE}
        self.aside = spread(late)
        self.child = (spread({key: z - a for key, (a, z) in first.items() if key not in LATE}), second)
        self.near = (
            spread({("p", 3): w, ("c", 3): 8 * rows[3]}),
            spread({("own", 3, 2): r, ("sib", 3, 2): r, ("own", 3, 1): r, **{("c", 2, y): 4 * rows[2] for y in (0, 1)}}),
        )
        self.far = (
            spread({("p", 2): w, ("p", 1): w, ("c", 1): 8 * rows[1]}),
            spread({("sib", 3, 1): r, ("g", 2, 1): r}),
        )
        self.before_3 = (
            spread(
                {
                    **{(side, k): w for k in (3, 2, 1) for side in ("own", "sib")},
                    "w4": w,
                    ("own", "c"): 8 * rows[3],
                    ("sib", "c"): 8 * rows[3],
                }
            ),
            spread(
                {
                    **{("own", 3, k): r for k in (2, 1)},
                    **{("sib", 3, k): r for k in (2, 1)},
                    ("c", 2): 16 * rows[2],
                }
            ),
        )
        self.after_3 = spread({("p", 2): w, ("p", 1): w, "spare": PAD})

    @staticmethod
    def total(pair):
        return max(pair[0][1], pair[1][1])


def swap(x, even, odd):
    size = lax.axis_size("pts")
    return lax.ppermute(x, "pts", [(i, i ^ (1 << (odd if i & 1 else even))) for i in range(size)])


def index_bit(bit):
    return lax.axis_index("pts") >> bit & 1


def by_role(first, second):
    role = index_bit(0)
    pl.when(role == 0)(first)
    pl.when(role == 1)(second)


def first_kernel(spans, rank, width, chunks, in_kernel, x_hbm, *refs):
    b_hbm = dict(zip(("r1", "r2", "s4", "s3", "s2", "r3", "r4"), refs[:7]))
    c_hbm = dict(zip(LEVELS, refs[7:11])) if in_kernel else {}
    refs = refs[7 + len(c_hbm) :]
    keep, send, x_v, left_v, right_v, acc_lo, acc_hi, acc_2, sems, c_sem = refs[:10]
    c_v = dict(zip(LEVELS, refs[10:]))
    points = x_v.shape[1]
    cut = points // chunks
    place = {"s4": (left_v, width), "s3": (left_v, width + rank), "s2": (left_v, width + 2 * rank)}
    place.update({name: (right_v, i * rank) for i, name in enumerate(("r1", "r2", "r3", "r4"))})

    def piece(j, i, name):
        cols = pl.ds(j * cut, cut)
        if name == "x":
            return pltpu.make_async_copy(x_hbm.at[:, cols], x_v.at[:, cols], sems.at[j, i])
        ref, row = place[name]
        return pltpu.make_async_copy(b_hbm[name].at[:, cols], ref.at[pl.ds(row, rank), cols], sems.at[j, i])

    copies = [[piece(j, i, n) for i, n in enumerate(("x", *b_hbm))] for j in range(chunks)]
    c_copies = [pltpu.make_async_copy(c_hbm[k], c_v[k], c_sem.at[i]) for i, k in enumerate(c_hbm)]
    for copy in copies[0] + c_copies:
        copy.start()
    for group in copies[1:]:
        for copy in group:
            copy.start()

    def add(j, ref, value):
        ref[...] = value if j == 0 else ref[...] + value

    for j in range(chunks):
        for copy in copies[j]:
            copy.wait()
        cols = slice(j * cut, (j + 1) * cut)
        left_v[:width, cols] = x_v[:, cols].astype(BF)
        add(j, acc_lo, nt(left_v[: width + 2 * rank, cols], right_v[: 2 * rank, cols]))
        add(j, acc_hi, nt(left_v[: width + rank, cols], right_v[2 * rank :, cols]))
        add(j, acc_2, nt(left_v[width + 2 * rank :, cols], right_v[:rank, cols]))
    for copy in c_copies:
        copy.wait()

    def write(role_0, role_1):
        def put(key, value):
            for out, table in zip((role_0, role_1), spans):
                if key in table:
                    out[table[key][0] : table[key][1]] = value.astype(BF)

        for i in range(2):
            side = slice(i * rank, (i + 1) * rank)
            put(("p", 1 + i), acc_lo[:width, side])
            put(("p", 3 + i), acc_hi[:width, side])
            put(("g", 4, 1 + i), acc_lo[width : width + rank, side])
            put(("g", 3, 1 + i), acc_lo[width + rank :, side])
        put(("g", 4, 3), acc_hi[width:, :rank])
        put(("g", 2, 1), acc_2[...])
        for k, ref in c_v.items():
            c = ref[...]
            put(("c", k), jnp.concatenate([c[:, :rank], c[:, rank:]], axis=0))

    by_role(lambda: write(keep, send), lambda: write(send, keep))


def interleave(first, second):
    half = first.shape[0] // 2
    if half % 16:
        first, second = first.astype(F32), second.astype(F32)
    parts = [first[:half], second[:half], first[half:], second[half:]]
    return jnp.concatenate(parts, axis=0).astype(BF)


def ordered(own, other, upper):
    return jnp.where(upper, other, own), jnp.where(upper, own, other)


def plus(a, z):
    return (a.astype(F32) + z.astype(F32)).astype(BF)


def merge_kernel(plan, keep, got, out, aside):
    def merge(role):
        for key, (lo, hi) in plan.device[role][0].items():
            a, z = keep[lo:hi], got[lo:hi]
            if key[0] == "c":
                value = interleave(z, a) if role else interleave(a, z)
            else:
                value = plus(a, z)
            late = role == 0 and key in LATE
            lo, hi = (plan.aside if late else plan.child[role])[0][key]
            (aside if late else out)[lo:hi] = value
        if role:
            aside[...] = jnp.zeros_like(aside)

    by_role(lambda: merge(0), lambda: merge(1))


def solve(stacked, own_rows, sib_rows, rank):
    sides = [jnp.concatenate([c[:rank], c[rank:]], axis=1) for c in (own_rows, sib_rows)]
    return nt(stacked, jnp.concatenate(sides, axis=0)).astype(BF)


def effect(weights, own_gram, sib_gram):
    gram = [jnp.concatenate([a, z], axis=0) for a, z in zip(own_gram, sib_gram)]
    return nn(weights, jnp.concatenate(gram, axis=1))


def transfer(rows, gram, rank):
    return jnp.concatenate([tn(rows[:rank], gram), tn(rows[rank:], gram)], axis=0)


def kernel_4(plan, bits, rank, own, got, after, near, far, weights):
    del after

    def first():
        spans = plan.child[0][0]

        def both(key):
            lo, hi = spans[key]
            return own[lo:hi], got[lo:hi]

        upper = index_bit(bits - 4) == 1
        stacked = jnp.concatenate(ordered(*both(("p", 4)), upper), axis=1)
        w = solve(stacked, *both(("c", 4)), rank)
        weights[...] = w
        a, z = both(("g", 4, 3))
        change = effect(w, [a], [z])
        a, z = both(("p", 3))
        lo, hi = plan.near[0][0][("p", 3)]
        near[lo:hi] = (a.astype(F32) + z.astype(F32) - change).astype(BF)
        for key, out, then in ((("c", 3), near, plan.near[0][0]), (("c", 1), far, plan.far[0][0])):
            lo, hi = then[key]
            out[lo:hi] = interleave(*ordered(*both(key), upper))

    def second():
        spans = plan.child[1][0]
        upper = index_bit(bits - 3) == 1

        def put(key, value):
            for out, then in ((near, plan.near[1][0]), (far, plan.far[1][0])):
                if key in then:
                    out[then[key][0] : then[key][1]] = value

        for key, (lo, hi) in spans.items():
            a, z = own[lo:hi], got[lo:hi]
            if key[0] == "c":
                for y, value in enumerate(ordered(a, z, upper)):
                    put(("c", key[1], y), value)
            elif key[1] == 3:
                put(("own", *key[1:]), a)
                put(("sib", *key[1:]), z)
            else:
                put(key, plus(a, z))
        weights[...] = jnp.zeros_like(weights)

    by_role(first, second)


def place_kernel(plan, bits, rank, before, own, got, weights, out):
    del before

    def first():
        def both(key):
            lo, hi = plan.aside[0][key]
            return own[lo:hi], got[lo:hi]

        def put(key, value):
            lo, hi = plan.far[0][0][key]
            out[lo:hi] = value

        below = (2, 1)
        pairs = [both(("g", 4, k)) for k in below]
        change = effect(weights[...], [p[0] for p in pairs], [p[1] for p in pairs])
        for i, k in enumerate(below):
            a, z = both(("p", k))
            put(("p", k), (a.astype(F32) + z.astype(F32) - change[:, i * rank : (i + 1) * rank]).astype(BF))

    pl.when(index_bit(0) == 0)(first)


def gather_kernel(plan, bits, rank, own_n, got_n, own_f, got_f, weights, out, gram):
    def keys(role):
        return (*plan.near[role][0], *plan.far[role][0])

    def both(role, key):
        if key in plan.near[role][0]:
            lo, hi = plan.near[role][0][key]
            return own_n[lo:hi], got_n[lo:hi]
        lo, hi = plan.far[role][0][key]
        return own_f[lo:hi], got_f[lo:hi]

    def first():
        then = plan.before_3[0][0]
        for key in keys(0):
            if key != ("c", 1):
                for side, value in zip(("own", "sib"), both(0, key)):
                    to = then[(side, "c" if key[0] == "c" else key[1])]
                    out[to[0] : to[1]] = value
        out[then["w4"][0] : then["w4"][1]] = weights[:, :rank]
        gram[...] = interleave(*ordered(*both(0, ("c", 1)), index_bit(bits - 3) == 1))

    def second():
        then = plan.before_3[1][0]
        upper = index_bit(bits - 4) == 1
        for key in keys(1):
            if key[0] != "c":
                value = plus(*both(1, key))
                if key in then:
                    out[then[key][0] : then[key][1]] = value
                else:
                    gram[...] = value
        rows = [interleave(*ordered(*both(1, ("c", 2, y)), upper)) for y in (0, 1)]
        to = then[("c", 2)]
        out[to[0] : to[1]] = interleave(*rows)

    by_role(first, second)


def early_z_kernel(plan, rank, own, gram, out):
    def first():
        out[:rank] = gram[...]
        out[rank:] = jnp.zeros_like(gram)

    def second():
        lo, hi = plan.before_3[1][0][("c", 2)]
        out[...] = transfer(own[lo:hi], gram[...], rank).astype(BF)

    by_role(first, second)


def meet_z_kernel(bits, rank, own, got, after, *outs):
    del after
    upper = index_bit(bits - 2) == 1

    def put(value):
        for out, rows in zip(outs, (value[:rank], value[rank:])):
            out[...] = rows

    def first():
        put(interleave(*ordered(own[:rank], got[:rank], upper)))

    def second():
        put(plus(own[...], got[...]))

    by_role(first, second)


def shared(mine, other, role):
    own, theirs = [jnp.concatenate([ref[...] for ref in refs], axis=0) for refs in (mine, other)]
    return jnp.where(index_bit(0) == role, own, theirs)


def kernel_3(plan, bits, rank, own, got, after, out, w4, w3, c2):
    del after

    def run(a_ref, b_ref):
        a_spans, b_spans, then = plan.before_3[0][0], plan.before_3[1][0], plan.after_3[0]

        def a(key):
            return a_ref[a_spans[key][0] : a_spans[key][1]]

        def b(key):
            return b_ref[b_spans[key][0] : b_spans[key][1]]

        def put(key, value):
            out[then[key][0] : then[key][1]] = value

        upper = index_bit(bits - 3) == 1
        stacked = jnp.concatenate(ordered(a(("own", 3)), a(("sib", 3)), upper), axis=1)
        w = solve(stacked, a(("own", "c")), a(("sib", "c")), rank)
        put("spare", jnp.zeros((PAD, rank), BF))
        w3[...] = w[:, :rank]
        w4[...] = a("w4")
        below = (2, 1)
        change = effect(w, [b(("own", 3, k)) for k in below], [b(("sib", 3, k)) for k in below])
        for i, k in enumerate(below):
            total = a(("own", k)).astype(F32) + a(("sib", k)).astype(F32)
            put(("p", k), (total - change[:, i * rank : (i + 1) * rank]).astype(BF))
        c2[...] = b(("c", 2))

    by_role(lambda: run(own, got), lambda: run(got, own))


def kernel_2(plan, bits, own, got, m0, m1, o0, o1, out, stacked_out):
    spans = plan.after_3[0]

    def both(key):
        lo, hi = spans[key]
        return own[lo:hi], got[lo:hi]

    stacked = jnp.concatenate(ordered(*both(("p", 2)), index_bit(bits - 2) == 1), axis=1)
    stacked_out[...] = stacked
    effect_1 = shared((m0, m1), (o0, o1), 1)
    a, z = both(("p", 1))
    out[...] = (a.astype(F32) + z.astype(F32) - nn(stacked, effect_1)).astype(BF)


def fetch_kernel(after, *refs):
    del after
    half = len(refs) // 2
    sems = refs[-1]
    copies = [pltpu.make_async_copy(a, z, sems.at[i]) for i, (a, z) in enumerate(zip(refs[:half], refs[half:-1]))]
    for copy in copies:
        copy.start()
    for copy in copies:
        copy.wait()


def early_kernel(rest, s4, s3, w4, w3, out):
    out[...] = rest[...] - nn(w4[...], s4[...]) - nn(w3[...], s3[...])


def middle_kernel(rest, s2, stacked, rows, out):
    rank = s2.shape[0]
    weights = nt(stacked[...], jnp.concatenate([rows[:rank], rows[rank:]], axis=1)).astype(BF)
    out[...] = rest[...] - nn(weights, s2[...])


def basis_kernel(m0, m1, o0, o1, s1, out):
    rank = m0.shape[0]
    c = shared((m0, m1), (o0, o1), 0)
    out[:rank] = tn(c[:rank], s1[...]).astype(BF)
    out[rank:] = tn(c[rank:], s1[...]).astype(BF)


def last_kernel(bits, chunks, own, got, rest, basis, out_hbm, out_v, sems):
    upper = index_bit(bits - 1) == 1
    stacked = jnp.concatenate(ordered(own[...], got[...], upper), axis=1)
    cut = rest.shape[1] // chunks
    copies = []
    for j in range(chunks):
        cols = slice(j * cut, (j + 1) * cut)
        out_v[:, cols] = rest[:, cols] - nn(stacked, basis[:, cols])
        span = pl.ds(j * cut, cut)
        copies.append(pltpu.make_async_copy(out_v.at[:, span], out_hbm.at[:, span], sems.at[j]))
        copies[-1].start()
    for copy in copies:
        copy.wait()


def on_device(right_solved, s1, s2, s3, s4, r1, r2, r3, r4, c1, c2, c3, c4):
    coupling = {1: c1, 2: c2, 3: c3, 4: c4}
    rank, points = s1.shape
    width = right_solved.shape[0]
    bits = lax.axis_size("pts").bit_length() - 1
    params = pltpu.CompilerParams(vmem_limit_bytes=24 * 2**20)

    def stay(x):
        return pltpu.with_memory_space_constraint(x, pltpu.HBM)

    def cost(flops, moved):
        return pl.CostEstimate(flops=flops, bytes_accessed=moved, transcendentals=0)

    def vmem_call(kernel, operands, shapes, name, **more):
        return pl.pallas_call(
            kernel,
            out_shape=shapes,
            in_specs=[VMEM] * len(operands),
            out_specs=[VMEM] * len(shapes),
            compiler_params=params,
            name=name,
            **more,
        )(*operands)

    def buffer(size):
        return jax.ShapeDtypeStruct((size, rank), BF)

    child_bits = bits - 4
    rows = {k: coupling[k].shape[0] for k in LEVELS}
    in_kernel = child_bits == 1 and all(rows[k] % 8 == 0 for k in LEVELS)
    if not in_kernel:
        rows = {k: rows[k] << child_bits - 1 for k in LEVELS}
    plan = Plan(width, rank, rows)
    device = plan.device
    if not in_kernel:
        device = tuple(spread({k: z - a for k, (a, z) in t.items() if k[0] != "c"}) for t, _ in device)
    operands = [right_solved, r1, r2, s4, s3, s2, r3, r4]
    if in_kernel:
        operands += [coupling[k] for k in LEVELS]
    chunks = CHUNKS_IN
    keep, send = pl.pallas_call(
        lambda *refs: first_kernel([t for t, _ in device], rank, width, chunks, in_kernel, *refs),
        out_shape=[buffer(Plan.total(device))] * 2,
        in_specs=[HBM] * len(operands),
        out_specs=[VMEM] * 2,
        scratch_shapes=[
            pltpu.VMEM((width, points), F32),
            pltpu.VMEM((width + 3 * rank, points), BF),
            pltpu.VMEM((4 * rank, points), BF),
            pltpu.VMEM((width + 2 * rank, 2 * rank), F32),
            pltpu.VMEM((width + rank, 2 * rank), F32),
            pltpu.VMEM((rank, rank), F32),
            pltpu.SemaphoreType.DMA((chunks, 8)),
            pltpu.SemaphoreType.DMA((4,)),
        ]
        + ([pltpu.VMEM(coupling[k].shape, F32) for k in LEVELS] if in_kernel else []),
        compiler_params=params,
        name="products",
    )(*[stay(x) for x in operands])

    size = Plan.total(plan.child)
    if in_kernel:
        got = swap(send, 0, 0)
        shapes = [buffer(size), buffer(plan.aside[1])]
        buf, aside = vmem_call(functools.partial(merge_kernel, plan), (keep, got), shapes, "merge")
    else:
        both = jnp.stack([keep, send])
        parts = {k: jnp.stack([c[:, :rank], c[:, rank:]]).astype(BF) for k, c in coupling.items()}
        both = plus(both, swap(both[::-1], 0, 0))
        both = jnp.where(index_bit(0) == 1, both[::-1], both)
        for bit in range(child_bits):
            if bit:
                both = plus(both, swap(both, bit, bit))
            upper = index_bit(bit) == 1
            for k in LEVELS:
                got = swap(parts[k], bit, bit)
                parts[k] = jnp.concatenate(ordered(parts[k], got, upper), axis=1)
        pieces = [{}, {}]
        for role in (0, 1):
            for key, (lo, hi) in device[role][0].items():
                pieces[role][key] = both[role, lo:hi]
            for k in SHARES[role]:
                pieces[role][("c", k)] = parts[k].reshape(-1, rank)
        shares = [jnp.concatenate([pieces[role][k] for k in plan.child[role][0]], axis=0) for role in (0, 1)]
        shares = [jnp.pad(x, ((0, size - x.shape[0]), (0, 0))) for x in shares]
        buf = jnp.where(index_bit(0) == 1, shares[1], shares[0])
        aside = jnp.concatenate([pieces[0][k] for k in plan.aside[0]], axis=0)

    weight = jax.ShapeDtypeStruct((width, rank), BF)
    wide = jax.ShapeDtypeStruct((width, points), F32)
    base = jax.ShapeDtypeStruct((rank, points), BF)
    got = swap(buf, bits - 4, bits - 3)
    got_aside = swap(aside, bits - 4, bits - 3)
    rest, s4_v, s3_v, s2_v, s1_v = pl.pallas_call(
        fetch_kernel,
        out_shape=[wide] + [base] * 4,
        in_specs=[VMEM] + [HBM] * 5,
        out_specs=[VMEM] * 5,
        scratch_shapes=[pltpu.SemaphoreType.DMA((5,))],
        compiler_params=params,
        cost_estimate=cost(0, 4 * width * points + 8 * rank * points),
        name="fetch",
    )(buf, *[stay(x) for x in (right_solved, s4, s3, s2, s1)])
    both_weights = jax.ShapeDtypeStruct((width, 2 * rank), BF)
    shapes = [buffer(Plan.total(plan.near)), buffer(Plan.total(plan.far)), both_weights]
    near, far, weights = vmem_call(functools.partial(kernel_4, plan, bits, rank), (buf, got, s1_v), shapes, "level_4")
    got_near = swap(near, bits - 3, bits - 4)
    place = functools.partial(place_kernel, plan, bits, rank)
    operands = (far, aside, got_aside, weights)
    (far,) = vmem_call(place, operands, [buffer(Plan.total(plan.far))], "place", input_output_aliases={0: 0})
    got_far = swap(far, bits - 3, bits - 4)
    shapes = [buffer(Plan.total(plan.before_3)), buffer(rank)]
    operands = (near, got_near, far, got_far, weights)
    buf, gram = vmem_call(functools.partial(gather_kernel, plan, bits, rank), operands, shapes, "gather")
    got = swap(buf, 0, 0)
    (own_z,) = vmem_call(functools.partial(early_z_kernel, plan, rank), (buf, gram), [buffer(2 * rank)], "early_z")
    got_z = swap(own_z, bits - 2, bits - 2)
    shapes = [buffer(plan.after_3[1]), weight, weight, buffer(2 * rank)]
    buf, w4, w3, c2_v = vmem_call(functools.partial(kernel_3, plan, bits, rank), (buf, got, own_z), shapes, "level_3")

    got = swap(buf, bits - 2, bits - 2)
    flops, moved = 2 * width * rank * points, 8 * width * points
    (rest,) = vmem_call(early_kernel, (rest, s4_v, s3_v, w4, w3), [wide], "early", cost_estimate=cost(2 * flops, moved))
    meet_z = functools.partial(meet_z_kernel, bits, rank)
    met = vmem_call(meet_z, (own_z, got_z, w3), [buffer(rank)] * 2, "meet_z")
    met = [*met, *[swap(x, 0, 0) for x in met]]
    shapes = [buffer(width), jax.ShapeDtypeStruct((width, 2 * rank), BF)]
    buf, stacked = vmem_call(functools.partial(kernel_2, plan, bits), (buf, got, *met), shapes, "level_2")
    (rest,) = vmem_call(middle_kernel, (rest, s2_v, stacked, c2_v), [wide], "middle", cost_estimate=cost(flops, moved))
    wide_basis = jax.ShapeDtypeStruct((2 * rank, points), BF)
    (basis_1,) = vmem_call(basis_kernel, (*met, s1_v), [wide_basis], "basis_1", cost_estimate=cost(4 * rank * rank * points, 6 * rank * points))
    got = swap(buf, bits - 1, bits - 1)
    chunks = CHUNKS_OUT
    return pl.pallas_call(
        functools.partial(last_kernel, bits, chunks),
        out_shape=wide,
        in_specs=[VMEM] * 4,
        out_specs=HBM,
        scratch_shapes=[pltpu.VMEM(wide.shape, F32), pltpu.SemaphoreType.DMA((chunks,))],
        compiler_params=params,
        name="last",
    )(buf, got, rest, basis_1)


def solution(mesh):
    wide, tall = P(None, "pts"), P("pts", None)
    return jax.shard_map(
        on_device, mesh=mesh, in_specs=(wide,) * 9 + (tall,) * 4, out_specs=wide, check_vma=False
    )
```

```python
import functools

import jax
import jax.numpy as jnp
from jax import lax
from jax.experimental import pallas as pl
from jax.experimental.pallas import tpu as pltpu
from jax.sharding import PartitionSpec as P

BF = jnp.bfloat16
F32 = jnp.float32
LEVELS = (4, 3, 2, 1)
LATE = (("p", 2), ("p", 1), ("g", 4, 2), ("g", 4, 1), ("c", 1))
SHARES = ((4, 3, 1), (2,))
VMEM = pl.BlockSpec(memory_space=pltpu.VMEM)
HBM = pl.BlockSpec(memory_space=pltpu.HBM)
CHUNKS_IN = 2
PAD = 16
CHUNKS_OUT = 4


def nn(a, b):
    return lax.dot_general(a, b, (((1,), (0,)), ((), ())), preferred_element_type=F32)


def nt(a, b):
    return lax.dot_general(a, b, (((1,), (1,)), ((), ())), preferred_element_type=F32)


def tn(a, b):
    return lax.dot_general(a, b, (((0,), (0,)), ((), ())), preferred_element_type=F32)


def spread(sizes):
    out, start = {}, 0
    for key, size in sizes.items():
        out[key] = (start, start + size)
        start += size
    return out, start


class Plan:
    def __init__(self, width, rank, rows):
        w, r = width, rank

        def start(scale):
            first = {("p", k): w for k in LEVELS}
            first.update({("g", 4, k): r for k in (3, 2, 1)})
            first.update({("c", k): 2 * scale * rows[k] for k in SHARES[0]})
            second = {("g", l, k): r for l, k in ((3, 2), (3, 1), (2, 1))}
            second.update({("c", k): 2 * scale * rows[k] for k in SHARES[1]})
            return spread(first), spread(second)

        self.device = start(1)
        (first, _), second = start(2)
        late = {key: z - a for key, (a, z) in first.items() if key in LATE}
        self.aside = spread(late)
        self.child = (spread({key: z - a for key, (a, z) in first.items() if key not in LATE}), second)
        self.near = (
            spread({("p", 3): w, ("c", 3): 8 * rows[3]}),
            spread({("own", 3, 2): r, ("sib", 3, 2): r, ("own", 3, 1): r, **{("c", 2, y): 4 * rows[2] for y in (0, 1)}}),
        )
        self.far = (
            spread({("p", 2): w, ("p", 1): w, ("c", 1): 8 * rows[1]}),
            spread({("sib", 3, 1): r, ("g", 2, 1): r}),
        )
        self.before_3 = (
            spread(
                {
                    **{(side, k): w for k in (3, 2, 1) for side in ("own", "sib")},
                    "w4": w,
                    ("own", "c"): 8 * rows[3],
                    ("sib", "c"): 8 * rows[3],
                }
            ),
            spread(
                {
                    **{("own", 3, k): r for k in (2, 1)},
                    **{("sib", 3, k): r for k in (2, 1)},
                    ("c", 2): 16 * rows[2],
                }
            ),
        )
        self.after_3 = spread({("p", 2): w, ("p", 1): w, "spare": PAD})

    @staticmethod
    def total(pair):
        return max(pair[0][1], pair[1][1])


def swap(x, even, odd):
    size = lax.axis_size("pts")
    return lax.ppermute(x, "pts", [(i, i ^ (1 << (odd if i & 1 else even))) for i in range(size)])


def index_bit(bit):
    return lax.axis_index("pts") >> bit & 1


def by_role(first, second):
    role = index_bit(0)
    pl.when(role == 0)(first)
    pl.when(role == 1)(second)


def first_kernel(spans, rank, width, chunks, in_kernel, x_hbm, *refs):
    b_hbm = dict(zip(("r1", "r2", "s4", "s3", "s2", "r3", "r4"), refs[:7]))
    c_hbm = dict(zip(LEVELS, refs[7:11])) if in_kernel else {}
    refs = refs[7 + len(c_hbm) :]
    keep, send, x_v, left_v, right_v, acc_lo, acc_hi, acc_2, sems, c_sem = refs[:10]
    c_v = dict(zip(LEVELS, refs[10:]))
    points = x_v.shape[1]
    cut = points // chunks
    place = {"s4": (left_v, width), "s3": (left_v, width + rank), "s2": (left_v, width + 2 * rank)}
    place.update({name: (right_v, i * rank) for i, name in enumerate(("r1", "r2", "r3", "r4"))})

    def piece(j, i, name):
        cols = pl.ds(j * cut, cut)
        if name == "x":
            return pltpu.make_async_copy(x_hbm.at[:, cols], x_v.at[:, cols], sems.at[j, i])
        ref, row = place[name]
        return pltpu.make_async_copy(b_hbm[name].at[:, cols], ref.at[pl.ds(row, rank), cols], sems.at[j, i])

    copies = [[piece(j, i, n) for i, n in enumerate(("x", *b_hbm))] for j in range(chunks)]
    c_copies = [pltpu.make_async_copy(c_hbm[k], c_v[k], c_sem.at[i]) for i, k in enumerate(c_hbm)]
    for copy in copies[0] + c_copies:
        copy.start()
    for group in copies[1:]:
        for copy in group:
            copy.start()

    def add(j, ref, value):
        ref[...] = value if j == 0 else ref[...] + value

    for j in range(chunks):
        for copy in copies[j]:
            copy.wait()
        cols = slice(j * cut, (j + 1) * cut)
        left_v[:width, cols] = x_v[:, cols].astype(BF)
        add(j, acc_lo, nt(left_v[: width + 2 * rank, cols], right_v[: 2 * rank, cols]))
        add(j, acc_hi, nt(left_v[: width + rank, cols], right_v[2 * rank :, cols]))
        add(j, acc_2, nt(left_v[width + 2 * rank :, cols], right_v[:rank, cols]))
    for copy in c_copies:
        copy.wait()

    def write(role_0, role_1):
        def put(key, value):
            for out, table in zip((role_0, role_1), spans):
                if key in table:
                    out[table[key][0] : table[key][1]] = value.astype(BF)

        for i in range(2):
            side = slice(i * rank, (i + 1) * rank)
            put(("p", 1 + i), acc_lo[:width, side])
            put(("p", 3 + i), acc_hi[:width, side])
            put(("g", 4, 1 + i), acc_lo[width : width + rank, side])
            put(("g", 3, 1 + i), acc_lo[width + rank :, side])
        put(("g", 4, 3), acc_hi[width:, :rank])
        put(("g", 2, 1), acc_2[...])
        for k, ref in c_v.items():
            c = ref[...]
            put(("c", k), jnp.concatenate([c[:, :rank], c[:, rank:]], axis=0))

    by_role(lambda: write(keep, send), lambda: write(send, keep))


def interleave(first, second):
    half = first.shape[0] // 2
    if half % 16:
        first, second = first.astype(F32), second.astype(F32)
    parts = [first[:half], second[:half], first[half:], second[half:]]
    return jnp.concatenate(parts, axis=0).astype(BF)


def ordered(own, other, upper):
    return jnp.where(upper, other, own), jnp.where(upper, own, other)


def plus(a, z):
    return (a.astype(F32) + z.astype(F32)).astype(BF)


def merge_kernel(plan, keep, got, out, aside):
    def merge(role):
        for key, (lo, hi) in plan.device[role][0].items():
            a, z = keep[lo:hi], got[lo:hi]
            if key[0] == "c":
                value = interleave(z, a) if role else interleave(a, z)
            else:
                value = plus(a, z)
            late = role == 0 and key in LATE
            lo, hi = (plan.aside if late else plan.child[role])[0][key]
            (aside if late else out)[lo:hi] = value
        if role:
            aside[...] = jnp.zeros_like(aside)

    by_role(lambda: merge(0), lambda: merge(1))


def solve(stacked, own_rows, sib_rows, rank):
    sides = [jnp.concatenate([c[:rank], c[rank:]], axis=1) for c in (own_rows, sib_rows)]
    return nt(stacked, jnp.concatenate(sides, axis=0)).astype(BF)


def effect(weights, own_gram, sib_gram):
    gram = [jnp.concatenate([a, z], axis=0) for a, z in zip(own_gram, sib_gram)]
    return nn(weights, jnp.concatenate(gram, axis=1))


def transfer(rows, gram, rank):
    return jnp.concatenate([tn(rows[:rank], gram), tn(rows[rank:], gram)], axis=0)


def kernel_4(plan, bits, rank, own, got, after, near, far, weights):
    del after

    def first():
        spans = plan.child[0][0]

        def both(key):
            lo, hi = spans[key]
            return own[lo:hi], got[lo:hi]

        upper = index_bit(bits - 4) == 1
        stacked = jnp.concatenate(ordered(*both(("p", 4)), upper), axis=1)
        w = solve(stacked, *both(("c", 4)), rank)
        weights[...] = w
        a, z = both(("g", 4, 3))
        change = effect(w, [a], [z])
        a, z = both(("p", 3))
        lo, hi = plan.near[0][0][("p", 3)]
        near[lo:hi] = (a.astype(F32) + z.astype(F32) - change).astype(BF)
        lo, hi = plan.near[0][0][("c", 3)]
        near[lo:hi] = interleave(*ordered(*both(("c", 3)), upper))

    def second():
        spans = plan.child[1][0]
        upper = index_bit(bits - 3) == 1

        def put(key, value):
            for out, then in ((near, plan.near[1][0]), (far, plan.far[1][0])):
                if key in then:
                    out[then[key][0] : then[key][1]] = value

        for key, (lo, hi) in spans.items():
            a, z = own[lo:hi], got[lo:hi]
            if key[0] == "c":
                for y, value in enumerate(ordered(a, z, upper)):
                    put(("c", key[1], y), value)
            elif key[1] == 3:
                put(("own", *key[1:]), a)
                put(("sib", *key[1:]), z)
            else:
                put(key, plus(a, z))
        weights[...] = jnp.zeros_like(weights)

    by_role(first, second)


def place_kernel(plan, bits, rank, before, own, got, weights, out):
    del before

    def first():
        def both(key):
            lo, hi = plan.aside[0][key]
            return own[lo:hi], got[lo:hi]

        def put(key, value):
            lo, hi = plan.far[0][0][key]
            out[lo:hi] = value

        below = (2, 1)
        pairs = [both(("g", 4, k)) for k in below]
        change = effect(weights[...], [p[0] for p in pairs], [p[1] for p in pairs])
        for i, k in enumerate(below):
            a, z = both(("p", k))
            put(("p", k), (a.astype(F32) + z.astype(F32) - change[:, i * rank : (i + 1) * rank]).astype(BF))
        put(("c", 1), interleave(*ordered(*both(("c", 1)), index_bit(bits - 4) == 1)))

    pl.when(index_bit(0) == 0)(first)


def gather_kernel(plan, bits, rank, own_n, got_n, own_f, got_f, weights, out, gram):
    def keys(role):
        return (*plan.near[role][0], *plan.far[role][0])

    def both(role, key):
        if key in plan.near[role][0]:
            lo, hi = plan.near[role][0][key]
            return own_n[lo:hi], got_n[lo:hi]
        lo, hi = plan.far[role][0][key]
        return own_f[lo:hi], got_f[lo:hi]

    def first():
        then = plan.before_3[0][0]
        for key in keys(0):
            if key != ("c", 1):
                for side, value in zip(("own", "sib"), both(0, key)):
                    to = then[(side, "c" if key[0] == "c" else key[1])]
                    out[to[0] : to[1]] = value
        out[then["w4"][0] : then["w4"][1]] = weights[:, :rank]
        gram[...] = interleave(*ordered(*both(0, ("c", 1)), index_bit(bits - 3) == 1))

    def second():
        then = plan.before_3[1][0]
        upper = index_bit(bits - 4) == 1
        for key in keys(1):
            if key[0] != "c":
                value = plus(*both(1, key))
                if key in then:
                    out[then[key][0] : then[key][1]] = value
                else:
                    gram[...] = value
        rows = [interleave(*ordered(*both(1, ("c", 2, y)), upper)) for y in (0, 1)]
        to = then[("c", 2)]
        out[to[0] : to[1]] = interleave(*rows)

    by_role(first, second)


def early_z_kernel(plan, rank, own, gram, out):
    def first():
        out[:rank] = gram[...]
        out[rank:] = jnp.zeros_like(gram)

    def second():
        lo, hi = plan.before_3[1][0][("c", 2)]
        out[...] = transfer(own[lo:hi], gram[...], rank).astype(BF)

    by_role(first, second)


def meet_z_kernel(bits, rank, own, got, after, *outs):
    del after
    upper = index_bit(bits - 2) == 1

    def put(value):
        for out, rows in zip(outs, (value[:rank], value[rank:])):
            out[...] = rows

    def first():
        put(interleave(*ordered(own[:rank], got[:rank], upper)))

    def second():
        put(plus(own[...], got[...]))

    by_role(first, second)


def shared(mine, other, role):
    own, theirs = [jnp.concatenate([ref[...] for ref in refs], axis=0) for refs in (mine, other)]
    return jnp.where(index_bit(0) == role, own, theirs)


def kernel_3(plan, bits, rank, own, got, after, out, w4, w3, c2):
    del after

    def run(a_ref, b_ref):
        a_spans, b_spans, then = plan.before_3[0][0], plan.before_3[1][0], plan.after_3[0]

        def a(key):
            return a_ref[a_spans[key][0] : a_spans[key][1]]

        def b(key):
            return b_ref[b_spans[key][0] : b_spans[key][1]]

        def put(key, value):
            out[then[key][0] : then[key][1]] = value

        upper = index_bit(bits - 3) == 1
        stacked = jnp.concatenate(ordered(a(("own", 3)), a(("sib", 3)), upper), axis=1)
        w = solve(stacked, a(("own", "c")), a(("sib", "c")), rank)
        put("spare", jnp.zeros((PAD, rank), BF))
        w3[...] = w[:, :rank]
        w4[...] = a("w4")
        below = (2, 1)
        change = effect(w, [b(("own", 3, k)) for k in below], [b(("sib", 3, k)) for k in below])
        for i, k in enumerate(below):
            total = a(("own", k)).astype(F32) + a(("sib", k)).astype(F32)
            put(("p", k), (total - change[:, i * rank : (i + 1) * rank]).astype(BF))
        c2[...] = b(("c", 2))

    by_role(lambda: run(own, got), lambda: run(got, own))


def kernel_2(plan, bits, own, got, m0, m1, o0, o1, out, stacked_out):
    spans = plan.after_3[0]

    def both(key):
        lo, hi = spans[key]
        return own[lo:hi], got[lo:hi]

    stacked = jnp.concatenate(ordered(*both(("p", 2)), index_bit(bits - 2) == 1), axis=1)
    stacked_out[...] = stacked
    effect_1 = shared((m0, m1), (o0, o1), 1)
    a, z = both(("p", 1))
    out[...] = (a.astype(F32) + z.astype(F32) - nn(stacked, effect_1)).astype(BF)


def fetch_kernel(after, *refs):
    del after
    half = len(refs) // 2
    sems = refs[-1]
    copies = [pltpu.make_async_copy(a, z, sems.at[i]) for i, (a, z) in enumerate(zip(refs[:half], refs[half:-1]))]
    for copy in copies:
        copy.start()
    for copy in copies:
        copy.wait()


def early_kernel(rest, s4, s3, w4, w3, out):
    out[...] = rest[...] - nn(w4[...], s4[...]) - nn(w3[...], s3[...])


def middle_kernel(rest, s2, stacked, rows, out):
    rank = s2.shape[0]
    weights = nt(stacked[...], jnp.concatenate([rows[:rank], rows[rank:]], axis=1)).astype(BF)
    out[...] = rest[...] - nn(weights, s2[...])


def basis_kernel(m0, m1, o0, o1, s1, out):
    rank = m0.shape[0]
    c = shared((m0, m1), (o0, o1), 0)
    out[:rank] = tn(c[:rank], s1[...]).astype(BF)
    out[rank:] = tn(c[rank:], s1[...]).astype(BF)


def last_kernel(bits, chunks, own, got, rest, basis, out_hbm, out_v, sems):
    upper = index_bit(bits - 1) == 1
    stacked = jnp.concatenate(ordered(own[...], got[...], upper), axis=1)
    cut = rest.shape[1] // chunks
    copies = []
    for j in range(chunks):
        cols = slice(j * cut, (j + 1) * cut)
        out_v[:, cols] = rest[:, cols] - nn(stacked, basis[:, cols])
        span = pl.ds(j * cut, cut)
        copies.append(pltpu.make_async_copy(out_v.at[:, span], out_hbm.at[:, span], sems.at[j]))
        copies[-1].start()
    for copy in copies:
        copy.wait()


def on_device(right_solved, s1, s2, s3, s4, r1, r2, r3, r4, c1, c2, c3, c4):
    coupling = {1: c1, 2: c2, 3: c3, 4: c4}
    rank, points = s1.shape
    width = right_solved.shape[0]
    bits = lax.axis_size("pts").bit_length() - 1
    params = pltpu.CompilerParams(vmem_limit_bytes=24 * 2**20)

    def stay(x):
        return pltpu.with_memory_space_constraint(x, pltpu.HBM)

    def cost(flops, moved):
        return pl.CostEstimate(flops=flops, bytes_accessed=moved, transcendentals=0)

    def vmem_call(kernel, operands, shapes, name, **more):
        return pl.pallas_call(
            kernel,
            out_shape=shapes,
            in_specs=[VMEM] * len(operands),
            out_specs=[VMEM] * len(shapes),
            compiler_params=params,
            name=name,
            **more,
        )(*operands)

    def buffer(size):
        return jax.ShapeDtypeStruct((size, rank), BF)

    child_bits = bits - 4
    rows = {k: coupling[k].shape[0] for k in LEVELS}
    in_kernel = child_bits == 1 and all(rows[k] % 8 == 0 for k in LEVELS)
    if not in_kernel:
        rows = {k: rows[k] << child_bits - 1 for k in LEVELS}
    plan = Plan(width, rank, rows)
    device = plan.device
    if not in_kernel:
        device = tuple(spread({k: z - a for k, (a, z) in t.items() if k[0] != "c"}) for t, _ in device)
    operands = [right_solved, r1, r2, s4, s3, s2, r3, r4]
    if in_kernel:
        operands += [coupling[k] for k in LEVELS]
    chunks = CHUNKS_IN
    keep, send = pl.pallas_call(
        lambda *refs: first_kernel([t for t, _ in device], rank, width, chunks, in_kernel, *refs),
        out_shape=[buffer(Plan.total(device))] * 2,
        in_specs=[HBM] * len(operands),
        out_specs=[VMEM] * 2,
        scratch_shapes=[
            pltpu.VMEM((width, points), F32),
            pltpu.VMEM((width + 3 * rank, points), BF),
            pltpu.VMEM((4 * rank, points), BF),
            pltpu.VMEM((width + 2 * rank, 2 * rank), F32),
            pltpu.VMEM((width + rank, 2 * rank), F32),
            pltpu.VMEM((rank, rank), F32),
            pltpu.SemaphoreType.DMA((chunks, 8)),
            pltpu.SemaphoreType.DMA((4,)),
        ]
        + ([pltpu.VMEM(coupling[k].shape, F32) for k in LEVELS] if in_kernel else []),
        compiler_params=params,
        name="products",
    )(*[stay(x) for x in operands])

    size = Plan.total(plan.child)
    if in_kernel:
        got = swap(send, 0, 0)
        shapes = [buffer(size), buffer(plan.aside[1])]
        buf, aside = vmem_call(functools.partial(merge_kernel, plan), (keep, got), shapes, "merge")
    else:
        both = jnp.stack([keep, send])
        parts = {k: jnp.stack([c[:, :rank], c[:, rank:]]).astype(BF) for k, c in coupling.items()}
        both = plus(both, swap(both[::-1], 0, 0))
        both = jnp.where(index_bit(0) == 1, both[::-1], both)
        for bit in range(child_bits):
            if bit:
                both = plus(both, swap(both, bit, bit))
            upper = index_bit(bit) == 1
            for k in LEVELS:
                got = swap(parts[k], bit, bit)
                parts[k] = jnp.concatenate(ordered(parts[k], got, upper), axis=1)
        pieces = [{}, {}]
        for role in (0, 1):
            for key, (lo, hi) in device[role][0].items():
                pieces[role][key] = both[role, lo:hi]
            for k in SHARES[role]:
                pieces[role][("c", k)] = parts[k].reshape(-1, rank)
        shares = [jnp.concatenate([pieces[role][k] for k in plan.child[role][0]], axis=0) for role in (0, 1)]
        shares = [jnp.pad(x, ((0, size - x.shape[0]), (0, 0))) for x in shares]
        buf = jnp.where(index_bit(0) == 1, shares[1], shares[0])
        aside = jnp.concatenate([pieces[0][k] for k in plan.aside[0]], axis=0)

    weight = jax.ShapeDtypeStruct((width, rank), BF)
    wide = jax.ShapeDtypeStruct((width, points), F32)
    base = jax.ShapeDtypeStruct((rank, points), BF)
    got = swap(buf, bits - 4, bits - 3)
    got_aside = swap(aside, bits - 4, bits - 3)
    rest, s4_v, s3_v, s2_v, s1_v = pl.pallas_call(
        fetch_kernel,
        out_shape=[wide] + [base] * 4,
        in_specs=[VMEM] + [HBM] * 5,
        out_specs=[VMEM] * 5,
        scratch_shapes=[pltpu.SemaphoreType.DMA((5,))],
        compiler_params=params,
        cost_estimate=cost(0, 4 * width * points + 8 * rank * points),
        name="fetch",
    )(buf, *[stay(x) for x in (right_solved, s4, s3, s2, s1)])
    both_weights = jax.ShapeDtypeStruct((width, 2 * rank), BF)
    shapes = [buffer(Plan.total(plan.near)), buffer(Plan.total(plan.far)), both_weights]
    near, far, weights = vmem_call(functools.partial(kernel_4, plan, bits, rank), (buf, got, s1_v), shapes, "level_4")
    got_near = swap(near, bits - 3, bits - 4)
    place = functools.partial(place_kernel, plan, bits, rank)
    operands = (far, aside, got_aside, weights)
    (far,) = vmem_call(place, operands, [buffer(Plan.total(plan.far))], "place", input_output_aliases={0: 0})
    got_far = swap(far, bits - 3, bits - 4)
    shapes = [buffer(Plan.total(plan.before_3)), buffer(rank)]
    operands = (near, got_near, far, got_far, weights)
    buf, gram = vmem_call(functools.partial(gather_kernel, plan, bits, rank), operands, shapes, "gather")
    got = swap(buf, 0, 0)
    (own_z,) = vmem_call(functools.partial(early_z_kernel, plan, rank), (buf, gram), [buffer(2 * rank)], "early_z")
    got_z = swap(own_z, bits - 2, bits - 2)
    shapes = [buffer(plan.after_3[1]), weight, weight, buffer(2 * rank)]
    buf, w4, w3, c2_v = vmem_call(functools.partial(kernel_3, plan, bits, rank), (buf, got, own_z), shapes, "level_3")

    got = swap(buf, bits - 2, bits - 2)
    flops, moved = 2 * width * rank * points, 8 * width * points
    (rest,) = vmem_call(early_kernel, (rest, s4_v, s3_v, w4, w3), [wide], "early", cost_estimate=cost(2 * flops, moved))
    meet_z = functools.partial(meet_z_kernel, bits, rank)
    met = vmem_call(meet_z, (own_z, got_z, w3), [buffer(rank)] * 2, "meet_z")
    met = [*met, *[swap(x, 0, 0) for x in met]]
    shapes = [buffer(width), jax.ShapeDtypeStruct((width, 2 * rank), BF)]
    buf, stacked = vmem_call(functools.partial(kernel_2, plan, bits), (buf, got, *met), shapes, "level_2")
    (rest,) = vmem_call(middle_kernel, (rest, s2_v, stacked, c2_v), [wide], "middle", cost_estimate=cost(flops, moved))
    wide_basis = jax.ShapeDtypeStruct((2 * rank, points), BF)
    (basis_1,) = vmem_call(basis_kernel, (*met, s1_v), [wide_basis], "basis_1", cost_estimate=cost(4 * rank * rank * points, 6 * rank * points))
    got = swap(buf, bits - 1, bits - 1)
    chunks = CHUNKS_OUT
    return pl.pallas_call(
        functools.partial(last_kernel, bits, chunks),
        out_shape=wide,
        in_specs=[VMEM] * 4,
        out_specs=HBM,
        scratch_shapes=[pltpu.VMEM(wide.shape, F32), pltpu.SemaphoreType.DMA((chunks,))],
        compiler_params=params,
        name="last",
    )(buf, got, rest, basis_1)


def solution(mesh):
    wide, tall = P(None, "pts"), P("pts", None)
    return jax.shard_map(
        on_device, mesh=mesh, in_specs=(wide,) * 9 + (tall,) * 4, out_specs=wide, check_vma=False
    )
```
